512 devices in a mesh: hull: 128 (over z, x, core), freq: 4 (over y).
Axes of the slice: x: 4, y: 4, z: 16, core: 2. Of those that a mesh axis runs over, the one named last changes fastest.
Arguments:
- wave_loads: bfloat16 [4, 128, 2, 36, 384], P('freq', 'hull'), may hold values from -0.47851562 to 0.47851562
- pivot_inverse: bfloat16 [4, 128, 2, 384, 384], P('freq', 'hull'), may hold values from -2.2 to 2.2
- forward_factor: bfloat16 [4, 128, 384], P('freq', 'hull'), may hold values from -1 to 1
- backward_factor: bfloat16 [4, 128, 384], P('freq', 'hull'), may hold values from -1 to 1
- recovery: bfloat16 [128, 256, 768], P('hull'), may hold values from -0.21875 to 0.21875
- hotspots: int32 [128, 256], P('hull'), may hold values from 0 to 255
- frequency: float32 [4], P('freq'), may hold values from 0.3 to 1.5
- spectrum: float32 [4, 36], P('freq'), may hold values from 0.1 to 7
Outputs:
- displacement: float32 [4, 128, 2, 36, 384], P('freq', 'hull')
- moments: float32 [3, 128, 36, 256], P(None, 'hull')
- log_damage: float32 [128, 36, 256], P('hull')
The draws below stay inside these ranges and needn't reach their ends.
All inputs are finite; a program needn't handle non-finite values.
Results may differ from the reference program's by a relative error of at most 0.0003.
Values may be sent and summed in bfloat16 or wider, within the bound.
No kernel may reach another device: no remote copies, remote signals or barrier semaphores. Data moves between devices by JAX's collectives and lax.ppermute only.
A program may use at most 64 MiB of HBM per device.

```python
import math
import jax
import jax.numpy as jnp
from jax import lax

INTERFACE_DOFS = 384
HEAD = 36
ELEM = 256
HS = 256
SEGMENT_COUNT = 128
FREQUENCY_COUNT = 4


def factor_law(key):
    random_subkeys = jax.random.split(key, 7)
    launch_layout = (FREQUENCY_COUNT, SEGMENT_COUNT, INTERFACE_DOFS)
    slow_share = 0.5
    slow_flag = jax.random.bernoulli(random_subkeys[0], slow_share, (FREQUENCY_COUNT, 1, INTERFACE_DOFS))
    gradual_rate = jnp.exp(-jax.random.uniform(random_subkeys[1], launch_layout, jnp.float32, 0.2, 0.8) / SEGMENT_COUNT)
    quick_rate = jnp.exp(-jax.random.uniform(random_subkeys[2], launch_layout, jnp.float32, 0.04, 0.09))
    surge_first = jax.random.randint(random_subkeys[3], (FREQUENCY_COUNT, 1, INTERFACE_DOFS), 0, SEGMENT_COUNT)
    surge_second = jax.random.randint(random_subkeys[4], (FREQUENCY_COUNT, 1, INTERFACE_DOFS), 0, SEGMENT_COUNT)
    segment_position = jnp.arange(SEGMENT_COUNT).reshape(1, SEGMENT_COUNT, 1)
    surge_falloff = jax.random.uniform(random_subkeys[5], launch_layout, jnp.float32, 0.5, 0.8)
    surge_amplitude = jnp.where((segment_position == surge_first) | (segment_position == surge_second), surge_falloff, 1.0)
    damping_rate = jnp.where(slow_flag, gradual_rate * surge_amplitude, quick_rate)
    signs = jnp.where(jax.random.bernoulli(random_subkeys[6], 0.5, launch_layout), 1.0, -1.0)
    return damping_rate * signs


def draw_forward_factor(key, part):
    return factor_law(jax.random.fold_in(key, 11)).astype(jnp.bfloat16)


def draw_backward_factor(key, part):
    return factor_law(jax.random.fold_in(key, 23)).astype(jnp.bfloat16)


def draw_pivot_inverse(key, part):
    random_subkeys = jax.random.split(jax.random.fold_in(key, 53), 3)
    launch_layout = (FREQUENCY_COUNT, SEGMENT_COUNT, INTERFACE_DOFS)
    pivot_scale = jax.random.uniform(random_subkeys[0], launch_layout, jnp.float32, 0.6, 1.4)
    angles = jax.random.uniform(random_subkeys[1], launch_layout, jnp.float32, -0.5, 0.5)
    diagonal = jnp.stack([pivot_scale * jnp.cos(angles), pivot_scale * jnp.sin(angles)], axis=2)
    unit_matrix = (jnp.arange(INTERFACE_DOFS)[:, None] == jnp.arange(INTERFACE_DOFS)[None, :]).astype(jnp.float32)
    coupling = jax.random.truncated_normal(random_subkeys[2], -3.0, 3.0, (FREQUENCY_COUNT, SEGMENT_COUNT, 2, INTERFACE_DOFS, INTERFACE_DOFS), jnp.float32) * 0.25
    return (coupling / math.sqrt(INTERFACE_DOFS) + diagonal[..., None] * unit_matrix).astype(jnp.bfloat16)


def draw_frequency(key, part):
    jitter = jax.random.uniform(jax.random.fold_in(key, 31), (FREQUENCY_COUNT,), jnp.float32, 0.25, 0.75)
    return 0.3 + 1.2 * (jnp.arange(FREQUENCY_COUNT).astype(jnp.float32) + jitter) / FREQUENCY_COUNT


def draw_spectrum(key, part):
    spread = jax.random.uniform(jax.random.fold_in(key, 41), (FREQUENCY_COUNT, HEAD), jnp.float32, -0.8, 0.8)
    rising = 0.4 + 1.6 * (jnp.arange(FREQUENCY_COUNT).astype(jnp.float32) + 0.5) / FREQUENCY_COUNT
    return rising[:, None] * jnp.exp(spread)


def plant(values, stream_key, smallest, high):
    extent = values.shape
    index_at = [jax.random.randint(jax.random.fold_in(stream_key, axis), (), 0, extent[axis]) for axis in range(len(extent))]
    values = values.at[tuple(index_at)].set(smallest)
    longest = extent.index(max(extent))
    index_at[longest] = (index_at[longest] + 1) % extent[longest]
    return values.at[tuple(index_at)].set(high)


def shard_levels(own_key, extent, cuts, least, largest):
    loudness, own = 1.0, jax.random.fold_in(own_key, 6)
    for position, blocks in cuts:
        heights = jnp.exp(jax.random.uniform(jax.random.fold_in(own, position), (blocks,), jnp.float32, least / len(cuts), largest / len(cuts)))
        loudness = loudness * jnp.repeat(heights, extent[position] // blocks).reshape([-1 if axis == position else 1 for axis in range(len(extent))])
    return loudness


def centred(rng, dims, scale, most, pieces=(), kind=jnp.bfloat16):
    loudness = shard_levels(rng, dims, pieces, -0.22, 0.18) if pieces else 1.0
    array = jax.random.normal(rng, dims, jnp.float32) * scale * loudness
    return jnp.minimum(jnp.maximum(array, -most), most).astype(kind)


def setup_inputs(seed: int = 0) -> dict:
    splits = jax.random.split(jax.random.key(seed), 9)
    wave_loads = centred(splits[0], (FREQUENCY_COUNT, SEGMENT_COUNT, 2, HEAD, INTERFACE_DOFS), 0.06, 0.47851562, ((0, 4), (1, 128)))
    pivot_inverse = draw_pivot_inverse(jax.random.fold_in(splits[8], 71), 0)
    forward_factor = draw_forward_factor(jax.random.fold_in(splits[8], 71), 0)
    backward_factor = draw_backward_factor(jax.random.fold_in(splits[8], 71), 0)
    recovery = centred(splits[4], (SEGMENT_COUNT, ELEM, 2 * INTERFACE_DOFS), (2 * INTERFACE_DOFS) ** -0.5, 0.21875, ((0, 128),))
    hotspots = plant(jax.random.randint(splits[5], (SEGMENT_COUNT, HS), 0, ELEM), jax.random.fold_in(splits[5], 1), 0, ELEM - 1).astype(jnp.int32)
    frequency = draw_frequency(jax.random.fold_in(splits[8], 71), 0)
    spectrum = draw_spectrum(jax.random.fold_in(splits[8], 71), 0)
    return {"wave_loads": wave_loads, "pivot_inverse": pivot_inverse, "forward_factor": forward_factor, "backward_factor": backward_factor, "recovery": recovery, "hotspots": hotspots, "frequency": frequency, "spectrum": spectrum}


precise = lax.Precision.HIGHEST

def complex_product(left_side, right_side):
    real_left = left_side[..., 0, :, :]
    imag_left = left_side[..., 1, :, :]
    real_right = right_side[..., 0, :, :]
    imag_right = right_side[..., 1, :, :]
    real_part = jnp.matmul(real_left, real_right, precision=precise) - jnp.matmul(imag_left, imag_right, precision=precise)
    imag_part = jnp.matmul(real_left, imag_right, precision=precise) + jnp.matmul(imag_left, real_right, precision=precise)
    return jnp.stack([real_part, imag_part], axis=-3)

def fatigue(moments):
    zeroth = moments[0]
    second = moments[1]
    fourth = moments[2]
    return 0.5 * jnp.log(fourth / second) + 1.5 * jnp.log(zeroth) + jnp.log(0.5 + 0.5 * second / jnp.sqrt(zeroth * fourth))

def reference(wave_loads, pivot_inverse, forward_factor, backward_factor, recovery, hotspots, frequency, spectrum):
    anchor = jnp.zeros((FREQUENCY_COUNT, 2, HEAD, INTERFACE_DOFS), jnp.float32)
    positions = jnp.arange(SEGMENT_COUNT, dtype=jnp.int32)

    def forward_step(front_now, segment_position):
        load_here = lax.dynamic_index_in_dim(wave_loads, segment_position, 1, False).astype(jnp.float32)
        pivot_here = lax.dynamic_index_in_dim(pivot_inverse, segment_position, 1, False).astype(jnp.float32)
        factor_here = lax.dynamic_index_in_dim(forward_factor, segment_position, 1, False).astype(jnp.float32)
        source = complex_product(load_here, pivot_here)
        front_new = source - front_now * factor_here[:, None, None, :]
        return (front_new, front_new)
    unused, fronts = lax.scan(forward_step, anchor, positions)

    def backward_step(motion_now, segment_position):
        factor_here = lax.dynamic_index_in_dim(backward_factor, segment_position, 1, False).astype(jnp.float32)
        front_here = lax.dynamic_index_in_dim(fronts, segment_position, 0, False)
        motion_new = front_here - motion_now * factor_here[:, None, None, :]
        return (motion_new, motion_new)
    unused, motions = lax.scan(backward_step, anchor, positions, reverse=True)
    sterns = jnp.concatenate([jnp.zeros((1, FREQUENCY_COUNT, 2, HEAD, INTERFACE_DOFS), jnp.float32), motions[:-1]], axis=0)

    def stress_one(segment_position):
        picked = jnp.take(recovery[segment_position], hotspots[segment_position], axis=0).astype(jnp.float32)
        aft_part = jnp.matmul(sterns[segment_position], picked[:, :INTERFACE_DOFS].T, precision=precise)
        bow_part = jnp.matmul(motions[segment_position], picked[:, INTERFACE_DOFS:].T, precision=precise)
        return aft_part + bow_part
    stress = lax.map(stress_one, positions)
    energy = stress[:, :, 0] ** 2 + stress[:, :, 1] ** 2
    weighted = (spectrum * (1.2 / FREQUENCY_COUNT))[None, :, :, None] * energy
    moments = jnp.stack([lax.optimization_barrier(jnp.sum(weighted * (frequency ** exponent)[None, :, None, None], axis=1)) for exponent in (0, 2, 4)])
    return (jnp.moveaxis(motions, 0, 1), moments, fatigue(moments))
```

```python
import jax
import jax.numpy as jnp
from jax import lax
from jax.experimental import pallas as pl
from jax.experimental.pallas import tpu as pltpu
from jax.sharding import Mesh, PartitionSpec as P

SPAN, PAIR, ACROSS, CORES = 8, 2, 4, 2
GROUP = PAIR * ACROSS * CORES
HEAD, MODES, POINTS = 36, 384, 256
HALF = 40
ROWS = 2 * HALF
SHARE = ROWS // GROUP
LANES = 128
TILES = MODES // LANES
INNER = ("zl", "x", "core")
F32 = jnp.float32
BF16 = jnp.bfloat16


def call(body, shapes, *args, vmem_mib=12, scratch=()):
    outs = [jax.ShapeDtypeStruct(shape, F32) for shape in shapes]
    return pl.pallas_call(
        body,
        out_shape=outs,
        in_specs=[pl.BlockSpec(memory_space=pltpu.VMEM)] * len(args),
        out_specs=[pl.BlockSpec(memory_space=pltpu.VMEM)] * len(outs),
        scratch_shapes=list(scratch),
        compiler_params=pltpu.CompilerParams(vmem_limit_bytes=vmem_mib * 2**20),
    )(*args)


def padded(rows):
    return jnp.concatenate([rows, jnp.zeros((HALF - HEAD, rows.shape[1]), rows.dtype)], axis=0)


def source_body(loads, pivot, forward, backward, out):
    real = padded(loads[0, 0, 0].astype(F32))
    imag = padded(loads[0, 0, 1].astype(F32))
    by_real = jnp.concatenate([real, imag], axis=0).astype(BF16)
    by_imag = jnp.concatenate([-imag, real], axis=0).astype(BF16)
    source = jnp.dot(by_real, pivot[0, 0, 0], preferred_element_type=F32) + jnp.dot(
        by_imag, pivot[0, 0, 1], preferred_element_type=F32
    )
    fore = -forward[...].astype(F32)
    back = -backward[...].astype(F32)
    blank = jnp.zeros((1, MODES), F32)
    for d in range(GROUP):
        out[d] = jnp.concatenate([source[SHARE * d : SHARE * (d + 1)], fore, back, blank], axis=0)


def reduce_body(got, out):
    front = got[0, 0:SHARE]
    gain = got[0, SHARE : SHARE + 1]
    fronts, gains = [front], [gain]
    for j in range(1, GROUP):
        fore = got[j, SHARE : SHARE + 1]
        front = got[j, 0:SHARE] + front * fore
        gain = gain * fore
        fronts.append(front)
        gains.append(gain)
    last_back = got[GROUP - 1, SHARE + 1 : SHARE + 2]
    motion, through, back_gain = front, gain, last_back
    for j in range(GROUP - 2, -1, -1):
        back = got[j, SHARE + 1 : SHARE + 2]
        motion = fronts[j] + motion * back
        through = gains[j] + through * back
        back_gain = back_gain * back
    blank = jnp.zeros((16 - 2 * SHARE - 4, MODES), F32)
    packed = jnp.concatenate([front, motion, gain, through, back_gain, last_back, blank], axis=0)
    for g in range(SPAN):
        out[g] = packed


def solve_body(place, got, ends, out, into, beyond, before):
    mine = place[0, 0]
    zero = jnp.zeros((SHARE, MODES), F32)
    into[0, 0:SHARE] = zero
    before[0, 0:1] = jnp.zeros((1, MODES), F32)
    arriving = [zero]
    for g in range(SPAN - 1):
        arriving.append(ends[g, 0:SHARE] + arriving[g] * ends[g, 2 * SHARE : 2 * SHARE + 1])
        into[g + 1, 0:SHARE] = arriving[g + 1]
        before[g + 1, 0:1] = ends[g, 2 * SHARE + 3 : 2 * SHARE + 4]
    returning = zero
    beyond[SPAN - 1, 0:SHARE] = zero
    for g in range(SPAN - 1, 0, -1):
        returning = (
            ends[g, SHARE : 2 * SHARE]
            + arriving[g] * ends[g, 2 * SHARE + 1 : 2 * SHARE + 2]
            + returning * ends[g, 2 * SHARE + 2 : 2 * SHARE + 3]
        )
        beyond[g - 1, 0:SHARE] = returning
    enter = into[mine, 0:SHARE]
    front = enter
    fronts = []
    for j in range(GROUP):
        front = got[j, 0:SHARE] + front * got[j, SHARE : SHARE + 1]
        fronts.append(front)
    motion = beyond[mine, 0:SHARE]
    motions = [None] * GROUP
    for j in range(GROUP - 1, -1, -1):
        motion = fronts[j] + motion * got[j, SHARE + 1 : SHARE + 2]
        motions[j] = motion
    previous = enter + motion * before[mine, 0:1]
    for j in range(GROUP):
        both = jnp.concatenate([motions[j], previous], axis=0)
        for t in range(TILES):
            out[j, 2 * SHARE * t : 2 * SHARE * (t + 1)] = both[:, LANES * t : LANES * (t + 1)]
        out[j, 2 * SHARE * TILES : 32] = jnp.zeros((32 - 2 * SHARE * TILES, LANES), F32)
        previous = motions[j]


def split(values, parts):
    pieces = []
    for _ in range(parts):
        piece = values.astype(BF16)
        values = values - piece.astype(F32)
        pieces.append(piece)
    return jnp.concatenate(pieces, axis=0)


def stress_body(got, recovery, hotspots, frequency, spectrum, motion_out, out, motion, stern):
    for d in range(GROUP):
        for t in range(TILES):
            lanes = slice(LANES * t, LANES * (t + 1))
            rows = slice(SHARE * d, SHARE * (d + 1))
            motion[rows, lanes] = got[d, 2 * SHARE * t : 2 * SHARE * t + SHARE]
            stern[rows, lanes] = got[d, 2 * SHARE * t + SHARE : 2 * SHARE * (t + 1)]
    motion_out[0, 0, 0] = motion[0:HEAD]
    motion_out[0, 0, 1] = motion[HALF : HALF + HEAD]
    contract = (((1,), (1,)), ((), ()))
    both = lax.dot_general(
        split(stern[...], 2), recovery[0, :, 0:MODES], contract, preferred_element_type=F32
    ) + lax.dot_general(
        split(motion[...], 2), recovery[0, :, MODES:], contract, preferred_element_type=F32
    )
    stress = both[0:ROWS] + both[ROWS:]
    power = stress[0:HALF] ** 2 + stress[HALF:] ** 2
    rows = lax.broadcasted_iota(jnp.int32, (HALF, HEAD), 0)
    columns = lax.broadcasted_iota(jnp.int32, (HALF, HEAD), 1)
    weight = jnp.sum(jnp.where(rows == columns, spectrum[...], 0.0), axis=1, keepdims=True)
    energy = power * (weight * (1.2 / 4))
    elements = lax.broadcasted_iota(jnp.int32, (POINTS, POINTS), 0)
    chosen = jnp.where(elements == hotspots[...], 1.0, 0.0).astype(BF16)
    thirds = jnp.dot(split(energy, 3), chosen, preferred_element_type=F32)
    energy = thirds[0:HALF] + (thirds[HALF : 2 * HALF] + thirds[2 * HALF :])
    here = jnp.broadcast_to(frequency[...], (1, POINTS))
    rows = lax.broadcasted_iota(jnp.int32, (HALF, POINTS), 0)
    packed = jnp.where(rows < HEAD, energy, here)
    for f in range(4):
        out[f] = packed


def damage_body(got, moments_out, damage_out):
    zeroth = jnp.zeros((HEAD, POINTS), F32)
    second = zeroth
    fourth = zeroth
    for f in range(4):
        energy = got[f, 0:HEAD]
        square = got[f, HEAD : HEAD + 1] ** 2
        zeroth = zeroth + energy
        second = second + energy * square
        fourth = fourth + energy * (square * square)
    moments_out[0, 0] = zeroth
    moments_out[1, 0] = second
    moments_out[2, 0] = fourth
    damage_out[0] = (
        0.5 * jnp.log(fourth / second)
        + 1.5 * jnp.log(zeroth)
        + jnp.log(0.5 + 0.5 * second / jnp.sqrt(zeroth * fourth))
    )


def exchange(values, axes):
    return lax.all_to_all(values, axes, 0, 0, tiled=True)


def per_device(wave_loads, pivot_inverse, forward, backward, recovery, hotspots, frequency, spectrum):
    place = jnp.reshape(lax.axis_index("zh"), (1, 1)).astype(jnp.int32)
    (source,) = call(
        source_body, [(GROUP, 8, MODES)], wave_loads, pivot_inverse, forward[0], backward[0]
    )
    shares = exchange(source, INNER)
    (ends,) = call(reduce_body, [(SPAN, 16, MODES)], shares)
    ends = exchange(ends, "zh")
    (solved,) = pl.pallas_call(
        solve_body,
        out_shape=[jax.ShapeDtypeStruct((GROUP, 32, LANES), F32)],
        in_specs=[
            pl.BlockSpec(memory_space=pltpu.SMEM),
            pl.BlockSpec(memory_space=pltpu.VMEM),
            pl.BlockSpec(memory_space=pltpu.VMEM),
        ],
        out_specs=[pl.BlockSpec(memory_space=pltpu.VMEM)],
        scratch_shapes=[pltpu.VMEM((SPAN, 8, MODES), F32)] * 3,
        compiler_params=pltpu.CompilerParams(vmem_limit_bytes=12 * 2**20),
    )(place, shares, ends)
    solved = exchange(solved, INNER)
    motion, energy = call(
        stress_body,
        [(1, 1, 2, HEAD, MODES), (4, HALF, POINTS)],
        solved,
        recovery,
        hotspots,
        frequency.reshape(1, 1),
        spectrum,
        scratch=[pltpu.VMEM((ROWS, MODES), F32)] * 2,
    )
    energy = exchange(energy, "freq")
    moments, damage = call(
        damage_body, [(3, 1, HEAD, POINTS), (1, HEAD, POINTS)], energy
    )
    return motion, moments, damage


def solution(mesh):
    cut = Mesh(mesh.devices.reshape(SPAN, PAIR, ACROSS, CORES, 4), ("zh",) + INNER + ("freq",))
    hull = ("zh",) + INNER
    in_specs = (
        P("freq", hull, None, None, None),
        P("freq", hull, None, None, None),
        P("freq", hull, None),
        P("freq", hull, None),
        P(hull, None, None),
        P(hull, None),
        P("freq"),
        P("freq", None),
    )
    out_specs = (
        P("freq", hull, None, None, None),
        P(None, hull, None, None),
        P(hull, None, None),
    )
    return jax.shard_map(per_device, mesh=cut, in_specs=in_specs, out_specs=out_specs, check_vma=False)
```

```python
import jax
import jax.numpy as jnp
from jax import lax
from jax.experimental import pallas as pl
from jax.experimental.pallas import tpu as pltpu
from jax.sharding import PartitionSpec as P

SPAN, GROUP = 8, 16
HEAD, MODES, POINTS = 36, 384, 256
HALF = 40
ROWS = 2 * HALF
SHARE = ROWS // GROUP
LANES = 128
TILES = MODES // LANES
NEAR = (4, 5, 6, 7, 8, 9, 10, 11, 12, 13, 14, 15, 0, 1, 2, 3)
FAR = (4, 5, 6, 7, 0, 1, 2, 3)
WAVES = (2, 3, 0, 1)
F32 = jnp.float32
BF16 = jnp.bfloat16


def call(body, shapes, *args, spaces=None, vmem_mib=12, scratch=()):
    outs = [jax.ShapeDtypeStruct(shape, F32) for shape in shapes]
    spaces = spaces or [pltpu.VMEM] * len(args)
    return pl.pallas_call(
        body,
        out_shape=outs,
        in_specs=[pl.BlockSpec(memory_space=space) for space in spaces],
        out_specs=[pl.BlockSpec(memory_space=pltpu.VMEM)] * len(outs),
        scratch_shapes=list(scratch),
        compiler_params=pltpu.CompilerParams(vmem_limit_bytes=vmem_mib * 2**20),
    )(*args)


def padded(rows):
    return jnp.concatenate([rows, jnp.zeros((HALF - HEAD, rows.shape[1]), rows.dtype)], axis=0)


def source_body(loads_hbm, pivot_hbm, forward_hbm, backward_hbm, out, loads, pivot, forward, backward, arrived):
    copies = [
        pltpu.make_async_copy(loads_hbm.at[0, 0], loads, arrived.at[0]),
        pltpu.make_async_copy(forward_hbm, forward, arrived.at[1]),
        pltpu.make_async_copy(backward_hbm, backward, arrived.at[2]),
        pltpu.make_async_copy(pivot_hbm.at[0, 0, 0], pivot.at[0], arrived.at[3]),
        pltpu.make_async_copy(pivot_hbm.at[0, 0, 1], pivot.at[1], arrived.at[4]),
    ]
    for copy in copies:
        copy.start()
    copies[0].wait()
    both = loads[...].astype(F32)
    real = padded(both[:, 0, :])
    imag = padded(both[:, 1, :])
    by_real = jnp.concatenate([real, imag], axis=0).astype(BF16)
    by_imag = jnp.concatenate([-imag, real], axis=0).astype(BF16)
    copies[1].wait()
    copies[2].wait()
    fore = -forward[...].astype(F32)
    back = -backward[...].astype(F32)
    copies[3].wait()
    source = jnp.dot(by_real, pivot[0], preferred_element_type=F32)
    copies[4].wait()
    source = source + jnp.dot(by_imag, pivot[1], preferred_element_type=F32)
    blank = jnp.zeros((1, MODES), F32)
    for d in range(GROUP):
        out[d] = jnp.concatenate([source[SHARE * d : SHARE * (d + 1)], fore, back, blank], axis=0)


def reduce_body(shares, out):
    got = [shares.at[NEAR.index(j)] for j in range(GROUP)]
    front = got[0][0:SHARE]
    gain = got[0][SHARE : SHARE + 1]
    fronts, gains = [front], [gain]
    for j in range(1, GROUP):
        fore = got[j][SHARE : SHARE + 1]
        front = got[j][0:SHARE] + front * fore
        gain = gain * fore
        fronts.append(front)
        gains.append(gain)
    last_back = got[GROUP - 1][SHARE + 1 : SHARE + 2]
    motion, through, back_gain = front, gain, last_back
    for j in range(GROUP - 2, -1, -1):
        back = got[j][SHARE + 1 : SHARE + 2]
        motion = fronts[j] + motion * back
        through = gains[j] + through * back
        back_gain = back_gain * back
    blank = jnp.zeros((16 - 2 * SHARE - 4, MODES), F32)
    packed = jnp.concatenate([front, motion, gain, through, back_gain, last_back, blank], axis=0)
    for g in range(SPAN):
        out[g] = packed


def solve_body(shares, reached, out, into, beyond, before):
    mine = lax.axis_index("hull") // GROUP
    got = [shares.at[NEAR.index(j)] for j in range(GROUP)]
    ends = [reached.at[FAR.index(g)] for g in range(SPAN)]
    zero = jnp.zeros((SHARE, MODES), F32)
    into[0, 0:SHARE] = zero
    before[0, 0:1] = jnp.zeros((1, MODES), F32)
    arriving = [zero]
    for g in range(SPAN - 1):
        arriving.append(ends[g][0:SHARE] + arriving[g] * ends[g][2 * SHARE : 2 * SHARE + 1])
        into[g + 1, 0:SHARE] = arriving[g + 1]
        before[g + 1, 0:1] = ends[g][2 * SHARE + 3 : 2 * SHARE + 4]
    returning = zero
    beyond[SPAN - 1, 0:SHARE] = zero
    for g in range(SPAN - 1, 0, -1):
        returning = (
            ends[g][SHARE : 2 * SHARE]
            + arriving[g] * ends[g][2 * SHARE + 1 : 2 * SHARE + 2]
            + returning * ends[g][2 * SHARE + 2 : 2 * SHARE + 3]
        )
        beyond[g - 1, 0:SHARE] = returning
    enter = into[mine, 0:SHARE]
    front = enter
    fronts = []
    for j in range(GROUP):
        front = got[j][0:SHARE] + front * got[j][SHARE : SHARE + 1]
        fronts.append(front)
    motion = beyond[mine, 0:SHARE]
    motions = [None] * GROUP
    for j in range(GROUP - 1, -1, -1):
        motion = fronts[j] + motion * got[j][SHARE + 1 : SHARE + 2]
        motions[j] = motion
    previous = enter + motion * before[mine, 0:1]
    for j in range(GROUP):
        both = jnp.concatenate([motions[j], previous], axis=0)
        for t in range(TILES):
            out[NEAR.index(j), 2 * SHARE * t : 2 * SHARE * (t + 1)] = both[:, LANES * t : LANES * (t + 1)]
        out[NEAR.index(j), 2 * SHARE * TILES : 32] = jnp.zeros((32 - 2 * SHARE * TILES, LANES), F32)
        previous = motions[j]


def split(values, parts):
    pieces = []
    for _ in range(parts):
        piece = values.astype(BF16)
        values = values - piece.astype(F32)
        pieces.append(piece)
    return jnp.concatenate(pieces, axis=0)


def stress_body(got, recovery, hotspots, frequency, spectrum, motion_out, out, motion, stern):
    for d in range(GROUP):
        for t in range(TILES):
            lanes = slice(LANES * t, LANES * (t + 1))
            rows = slice(SHARE * d, SHARE * (d + 1))
            motion[rows, lanes] = got[d, 2 * SHARE * t : 2 * SHARE * t + SHARE]
            stern[rows, lanes] = got[d, 2 * SHARE * t + SHARE : 2 * SHARE * (t + 1)]
    motion_out[0, 0, :, 0, :] = motion[0:HEAD]
    motion_out[0, 0, :, 1, :] = motion[HALF : HALF + HEAD]
    contract = (((1,), (1,)), ((), ()))
    both = lax.dot_general(
        split(stern[...], 2), recovery[0, :, 0:MODES], contract, preferred_element_type=F32
    ) + lax.dot_general(
        split(motion[...], 2), recovery[0, :, MODES:], contract, preferred_element_type=F32
    )
    stress = both[0:ROWS] + both[ROWS:]
    power = stress[0:HALF] ** 2 + stress[HALF:] ** 2
    rows = lax.broadcasted_iota(jnp.int32, (HALF, HEAD), 0)
    columns = lax.broadcasted_iota(jnp.int32, (HALF, HEAD), 1)
    weight = jnp.sum(jnp.where(rows == columns, spectrum[...], 0.0), axis=1, keepdims=True)
    energy = power * (weight * (1.2 / 4))
    elements = lax.broadcasted_iota(jnp.int32, (POINTS, POINTS), 0)
    chosen = jnp.where(elements == hotspots[...], 1.0, 0.0).astype(BF16)
    thirds = jnp.dot(split(energy, 3), chosen, preferred_element_type=F32)
    energy = thirds[0:HALF] + (thirds[HALF : 2 * HALF] + thirds[2 * HALF :])
    here = jnp.full((1, POINTS), frequency[0], F32)
    rows = lax.broadcasted_iota(jnp.int32, (HALF, POINTS), 0)
    packed = jnp.where(rows < HEAD, energy, here)
    for f in range(4):
        out[f] = packed


def damage_body(got, moments_out, damage_out):
    zeroth = jnp.zeros((HEAD, POINTS), F32)
    second = zeroth
    fourth = zeroth
    for f in range(4):
        energy = got[f, 0:HEAD]
        square = got[f, HEAD : HEAD + 1] ** 2
        zeroth = zeroth + energy
        second = second + energy * square
        fourth = fourth + energy * (square * square)
    moments_out[0, :, 0, :] = zeroth
    moments_out[1, :, 0, :] = second
    moments_out[2, :, 0, :] = fourth
    damage_out[:, 0, :] = (
        0.5 * jnp.log(fourth / second)
        + 1.5 * jnp.log(zeroth)
        + jnp.log(0.5 + 0.5 * second / jnp.sqrt(zeroth * fourth))
    )


def exchange(values, axis, groups):
    return lax.all_to_all(values, axis, 0, 0, axis_index_groups=groups, tiled=True)


def per_device(wave_loads, pivot_inverse, forward, backward, recovery, hotspots, frequency, spectrum):
    near = [[GROUP * g + j for j in NEAR] for g in range(SPAN)]
    far = [[GROUP * g + j for g in FAR] for j in range(GROUP)]
    (source,) = call(
        source_body,
        [(GROUP, 8, MODES)],
        jnp.transpose(wave_loads, (0, 1, 3, 2, 4)),
        pivot_inverse,
        forward[0],
        backward[0],
        spaces=[pl.ANY] * 4,
        vmem_mib=56,
        scratch=[
            pltpu.VMEM((HEAD, 2, MODES), BF16),
            pltpu.VMEM((2, MODES, MODES), BF16),
            pltpu.VMEM((1, MODES), BF16),
            pltpu.VMEM((1, MODES), BF16),
            pltpu.SemaphoreType.DMA((5,)),
        ],
    )
    shares = exchange(source, "hull", near)
    (ends,) = call(reduce_body, [(SPAN, 16, MODES)], shares)
    ends = exchange(ends, "hull", far)
    (solved,) = call(
        solve_body,
        [(GROUP, 32, LANES)],
        shares,
        ends,
        scratch=[pltpu.VMEM((SPAN, 8, MODES), F32)] * 3,
    )
    solved = exchange(solved, "hull", near)
    motion, energy = call(
        stress_body,
        [(1, 1, HEAD, 2, MODES), (4, HALF, POINTS)],
        solved,
        recovery,
        hotspots,
        frequency,
        spectrum,
        spaces=[pltpu.VMEM] * 3 + [pltpu.SMEM, pltpu.VMEM],
        scratch=[pltpu.VMEM((ROWS, MODES), F32)] * 2,
    )
    energy = exchange(energy, "freq", [WAVES])
    moments, damage = call(damage_body, [(3, HEAD, 1, POINTS), (HEAD, 1, POINTS)], energy)
    return (
        jnp.transpose(motion, (0, 1, 3, 2, 4)),
        jnp.transpose(moments, (0, 2, 1, 3)),
        jnp.transpose(damage, (1, 0, 2)),
    )


def solution(mesh):
    in_specs = (
        P("freq", "hull", None, None, None),
        P("freq", "hull", None, None, None),
        P("freq", "hull", None),
        P("freq", "hull", None),
        P("hull", None, None),
        P("hull", None),
        P("freq"),
        P("freq", None),
    )
    out_specs = (
        P("freq", "hull", None, None, None),
        P(None, "hull", None, None),
        P("hull", None, None),
    )
    return jax.shard_map(per_device, mesh=mesh, in_specs=in_specs, out_specs=out_specs, check_vma=False)
```

```python
import jax
import jax.numpy as jnp
from jax import lax
from jax.experimental import pallas as pl
from jax.experimental.pallas import tpu as pltpu
from jax.sharding import PartitionSpec as P

SPAN, GROUP = 8, 16
HEAD, MODES, POINTS = 36, 384, 256
HALF = 40
ROWS = 2 * HALF
SHARE = ROWS // GROUP
END = 2 * SHARE + 3
ENDS = 40
LANES = 128
TILES = MODES // LANES
NEAR = (15, 14, 13, 12, 11, 10, 9, 8, 7, 6, 5, 4, 3, 2, 1, 0)
BACK = (4, 5, 6, 7, 8, 9, 10, 11, 12, 13, 14, 15, 0, 1, 2, 3)
FAR = (5, 4, 6, 3, 7, 2, 0, 1)
WAVES = (3, 2, 1, 0)
F32 = jnp.float32
BF16 = jnp.bfloat16


def call(body, shapes, *args, spaces=None, vmem_mib=12, scratch=()):
    outs = [jax.ShapeDtypeStruct(shape, F32) for shape in shapes]
    spaces = spaces or [pltpu.VMEM] * len(args)
    return pl.pallas_call(
        body,
        out_shape=outs,
        in_specs=[pl.BlockSpec(memory_space=space) for space in spaces],
        out_specs=[pl.BlockSpec(memory_space=pltpu.VMEM)] * len(outs),
        scratch_shapes=list(scratch),
        compiler_params=pltpu.CompilerParams(vmem_limit_bytes=vmem_mib * 2**20),
    )(*args)


def padded(rows):
    return jnp.concatenate([rows, jnp.zeros((HALF - HEAD, rows.shape[1]), rows.dtype)], axis=0)


def source_body(loads_hbm, pivot_hbm, forward_hbm, backward_hbm, out, loads, pivot, forward, backward, arrived):
    copies = [
        pltpu.make_async_copy(loads_hbm.at[0, 0], loads, arrived.at[0]),
        pltpu.make_async_copy(forward_hbm, forward, arrived.at[1]),
        pltpu.make_async_copy(backward_hbm, backward, arrived.at[2]),
        pltpu.make_async_copy(pivot_hbm.at[0, 0, 0], pivot.at[0], arrived.at[3]),
        pltpu.make_async_copy(pivot_hbm.at[0, 0, 1], pivot.at[1], arrived.at[4]),
    ]
    for copy in copies:
        copy.start()
    copies[0].wait()
    both = loads[...].astype(F32)
    real = padded(both[:, 0, :])
    imag = padded(both[:, 1, :])
    by_real = jnp.concatenate([real, imag], axis=0).astype(BF16)
    by_imag = jnp.concatenate([-imag, real], axis=0).astype(BF16)
    copies[1].wait()
    copies[2].wait()
    fore = -forward[...].astype(F32)
    back = -backward[...].astype(F32)
    copies[3].wait()
    source = jnp.dot(by_real, pivot[0], preferred_element_type=F32)
    copies[4].wait()
    source = source + jnp.dot(by_imag, pivot[1], preferred_element_type=F32)
    blank = jnp.zeros((1, MODES), F32)
    for d in range(GROUP):
        out[d] = jnp.concatenate([source[SHARE * d : SHARE * (d + 1)], fore, back, blank], axis=0)


def reduce_body(shares, out):
    got = [shares.at[NEAR.index(j)] for j in range(GROUP)]
    front = got[0][0:SHARE]
    gain = got[0][SHARE : SHARE + 1]
    fronts, gains = [front], [gain]
    for j in range(1, GROUP):
        fore = got[j][SHARE : SHARE + 1]
        front = got[j][0:SHARE] + front * fore
        gain = gain * fore
        fronts.append(front)
        gains.append(gain)
    last_back = got[GROUP - 1][SHARE + 1 : SHARE + 2]
    motion, through, back_gain = front, gain, last_back
    for j in range(GROUP - 2, -1, -1):
        back = got[j][SHARE + 1 : SHARE + 2]
        motion = fronts[j] + motion * back
        through = gains[j] + through * back
        back_gain = back_gain * back
    mine = lax.axis_index("hull") // GROUP
    blank = jnp.zeros((ENDS - TILES * END, LANES), F32)
    for place in range(SPAN):
        third = jnp.where(mine < FAR[place], last_back, through)
        packed = jnp.concatenate([front, motion, gain, third, back_gain], axis=0)
        pieces = [packed[:, LANES * t : LANES * (t + 1)] for t in range(TILES)]
        out[place] = jnp.concatenate(pieces + [blank], axis=0)


def solve_body(shares, reached, recovery, hotspots, frequency, spectrum, out, into, beyond, before):
    mine = lax.axis_index("hull") // GROUP
    got = [shares.at[NEAR.index(j)] for j in range(GROUP)]
    ends = []
    for g in range(SPAN):
        packed = reached[FAR.index(g)]
        ends.append(jnp.concatenate([packed[END * t : END * (t + 1)] for t in range(TILES)], axis=1))
    zero = jnp.zeros((SHARE, MODES), F32)
    into[0, 0:SHARE] = zero
    before[0, 0:1] = jnp.zeros((1, MODES), F32)
    arriving = [zero]
    for g in range(SPAN - 1):
        arriving.append(ends[g][0:SHARE] + arriving[g] * ends[g][2 * SHARE : 2 * SHARE + 1])
        into[g + 1, 0:SHARE] = arriving[g + 1]
        before[g + 1, 0:1] = ends[g][2 * SHARE + 1 : 2 * SHARE + 2]
    returning = zero
    beyond[SPAN - 1, 0:SHARE] = zero
    for g in range(SPAN - 1, 0, -1):
        returning = (
            ends[g][SHARE : 2 * SHARE]
            + arriving[g] * ends[g][2 * SHARE + 1 : 2 * SHARE + 2]
            + returning * ends[g][2 * SHARE + 2 : 2 * SHARE + 3]
        )
        beyond[g - 1, 0:SHARE] = returning
    enter = into[mine, 0:SHARE]
    front = enter
    fronts = []
    for j in range(GROUP):
        front = got[j][0:SHARE] + front * got[j][SHARE : SHARE + 1]
        fronts.append(front)
    motion = beyond[mine, 0:SHARE]
    motions = [None] * GROUP
    for j in range(GROUP - 1, -1, -1):
        motion = fronts[j] + motion * got[j][SHARE + 1 : SHARE + 2]
        motions[j] = motion
    previous = enter + motion * before[mine, 0:1]
    for j in range(GROUP):
        both = jnp.concatenate([motions[j], previous], axis=0)
        for t in range(TILES):
            out[BACK.index(j), 2 * SHARE * t : 2 * SHARE * (t + 1)] = both[:, LANES * t : LANES * (t + 1)]
        out[BACK.index(j), 2 * SHARE * TILES : 32] = jnp.zeros((32 - 2 * SHARE * TILES, LANES), F32)
        previous = motions[j]


def split(values, parts):
    pieces = []
    for _ in range(parts):
        piece = values.astype(BF16)
        values = values - piece.astype(F32)
        pieces.append(piece)
    return jnp.concatenate(pieces, axis=0)


def stress_body(got, recovery, hotspots, frequency, spectrum, motion_out, out, motion, stern):
    for place in range(GROUP):
        d = NEAR.index(BACK[place])
        for t in range(TILES):
            lanes = slice(LANES * t, LANES * (t + 1))
            rows = slice(SHARE * d, SHARE * (d + 1))
            motion[rows, lanes] = got[place, 2 * SHARE * t : 2 * SHARE * t + SHARE]
            stern[rows, lanes] = got[place, 2 * SHARE * t + SHARE : 2 * SHARE * (t + 1)]
    motion_out[0, 0, :, 0, :] = motion[0:HEAD]
    motion_out[0, 0, :, 1, :] = motion[HALF : HALF + HEAD]
    contract = (((1,), (1,)), ((), ()))
    both = lax.dot_general(
        split(stern[...], 2), recovery[0, :, 0:MODES], contract, preferred_element_type=F32
    ) + lax.dot_general(
        split(motion[...], 2), recovery[0, :, MODES:], contract, preferred_element_type=F32
    )
    stress = both[0:ROWS] + both[ROWS:]
    power = stress[0:HALF] ** 2 + stress[HALF:] ** 2
    rows = lax.broadcasted_iota(jnp.int32, (HALF, HEAD), 0)
    columns = lax.broadcasted_iota(jnp.int32, (HALF, HEAD), 1)
    weight = jnp.sum(jnp.where(rows == columns, spectrum[...], 0.0), axis=1, keepdims=True)
    energy = power * (weight * (1.2 / 4))
    elements = lax.broadcasted_iota(jnp.int32, (POINTS, POINTS), 0)
    chosen = jnp.where(elements == hotspots[...], 1.0, 0.0).astype(BF16)
    thirds = jnp.dot(split(energy, 3), chosen, preferred_element_type=F32)
    energy = thirds[0:HALF] + (thirds[HALF : 2 * HALF] + thirds[2 * HALF :])
    here = jnp.broadcast_to(frequency[...].reshape(1, 1), (1, POINTS))
    rows = lax.broadcasted_iota(jnp.int32, (HALF, POINTS), 0)
    packed = jnp.where(rows < HEAD, energy, here)
    for f in range(4):
        out[f] = packed


def damage_body(got, moments_out, damage_out):
    zeroth = jnp.zeros((HEAD, POINTS), F32)
    second = zeroth
    fourth = zeroth
    for f in range(4):
        energy = got[f, 0:HEAD]
        square = got[f, HEAD : HEAD + 1] ** 2
        zeroth = zeroth + energy
        second = second + energy * square
        fourth = fourth + energy * (square * square)
    moments_out[0, :, 0, :] = zeroth
    moments_out[1, :, 0, :] = second
    moments_out[2, :, 0, :] = fourth
    damage_out[:, 0, :] = (
        0.5 * jnp.log(fourth / second)
        + 1.5 * jnp.log(zeroth)
        + jnp.log(0.5 + 0.5 * second / jnp.sqrt(zeroth * fourth))
    )


def exchange(values, axis, groups):
    return lax.all_to_all(values, axis, 0, 0, axis_index_groups=groups, tiled=True)


def per_device(wave_loads, pivot_inverse, forward, backward, recovery, hotspots, frequency, spectrum):
    near = [[GROUP * g + j for j in NEAR] for g in range(SPAN)]
    back = [[GROUP * g + j for j in BACK] for g in range(SPAN)]
    far = [[GROUP * g + j for g in FAR] for j in range(GROUP)]
    (source,) = call(
        source_body,
        [(GROUP, 8, MODES)],
        jnp.transpose(wave_loads, (0, 1, 3, 2, 4)),
        pivot_inverse,
        forward[0],
        backward[0],
        spaces=[pl.ANY] * 4,
        vmem_mib=56,
        scratch=[
            pltpu.VMEM((HEAD, 2, MODES), BF16),
            pltpu.VMEM((2, MODES, MODES), BF16),
            pltpu.VMEM((1, MODES), BF16),
            pltpu.VMEM((1, MODES), BF16),
            pltpu.SemaphoreType.DMA((5,)),
        ],
    )
    shares = exchange(source, "hull", near)
    (ends,) = call(reduce_body, [(SPAN, ENDS, LANES)], shares)
    ends = exchange(ends, "hull", far)
    (solved,) = call(
        solve_body,
        [(GROUP, 32, LANES)],
        shares,
        ends,
        recovery,
        hotspots,
        frequency,
        spectrum,
        scratch=[pltpu.VMEM((SPAN, 8, MODES), F32)] * 3,
    )
    solved = exchange(solved, "hull", back)
    motion, energy = call(
        stress_body,
        [(1, 1, HEAD, 2, MODES), (4, HALF, POINTS)],
        solved,
        recovery,
        hotspots,
        frequency,
        spectrum,
        scratch=[pltpu.VMEM((ROWS, MODES), F32)] * 2,
    )
    energy = exchange(energy, "freq", [WAVES])
    moments, damage = call(damage_body, [(3, HEAD, 1, POINTS), (HEAD, 1, POINTS)], energy)
    return (
        jnp.transpose(motion, (0, 1, 3, 2, 4)),
        jnp.transpose(moments, (0, 2, 1, 3)),
        jnp.transpose(damage, (1, 0, 2)),
    )


def solution(mesh):
    in_specs = (
        P("freq", "hull", None, None, None),
        P("freq", "hull", None, None, None),
        P("freq", "hull", None),
        P("freq", "hull", None),
        P("hull", None, None),
        P("hull", None),
        P("freq"),
        P("freq", None),
    )
    out_specs = (
        P("freq", "hull", None, None, None),
        P(None, "hull", None, None),
        P("hull", None, None),
    )
    return jax.shard_map(per_device, mesh=mesh, in_specs=in_specs, out_specs=out_specs, check_vma=False)
```

```python
import jax
import jax.numpy as jnp
from jax import lax
from jax.experimental import pallas as pl
from jax.experimental.pallas import tpu as pltpu
from jax.sharding import PartitionSpec as P

SPAN, GROUP = 8, 16
HEAD, MODES, POINTS = 36, 384, 256
LANES = 128
TILES = MODES // LANES
HALF = 40
PAD = HALF - HEAD
DEEP, FIVE = 14, 5
TAIL = 2 * HEAD - DEEP * FIVE
LAST = FIVE * TILES
ENDS = 32
NEAR = (15, 14, 13, 12, 11, 10, 9, 8, 7, 6, 5, 4, 3, 2, 1, 0)
BACK = (4, 5, 6, 7, 8, 9, 10, 11, 12, 13, 14, 15, 0, 1, 2, 3)
FAR = (5, 1, 0, 2, 7, 3, 6, 4)
WAVES = (3, 2, 1, 0)
F32 = jnp.float32
BF16 = jnp.bfloat16


def call(body, shapes, *args, spaces=None, vmem_mib=12, scratch=()):
    outs = [jax.ShapeDtypeStruct(shape, F32) for shape in shapes]
    spaces = spaces or [pltpu.VMEM] * len(args)
    return pl.pallas_call(
        body,
        out_shape=outs,
        in_specs=[pl.BlockSpec(memory_space=space) for space in spaces],
        out_specs=[pl.BlockSpec(memory_space=pltpu.VMEM)] * len(outs),
        scratch_shapes=list(scratch),
        compiler_params=pltpu.CompilerParams(vmem_limit_bytes=vmem_mib * 2**20),
    )(*args)


def padded(rows):
    return jnp.concatenate([rows, jnp.zeros((HALF - HEAD, rows.shape[1]), rows.dtype)], axis=0)


def source_body(loads_hbm, pivot_hbm, forward_hbm, backward_hbm, out, loads, pivot, forward, backward, arrived):
    copies = [
        pltpu.make_async_copy(loads_hbm.at[0, 0], loads, arrived.at[0]),
        pltpu.make_async_copy(forward_hbm, forward, arrived.at[1]),
        pltpu.make_async_copy(backward_hbm, backward, arrived.at[2]),
        pltpu.make_async_copy(pivot_hbm.at[0, 0, 0], pivot.at[0], arrived.at[3]),
        pltpu.make_async_copy(pivot_hbm.at[0, 0, 1], pivot.at[1], arrived.at[4]),
    ]
    for copy in copies:
        copy.start()
    copies[0].wait()
    both = loads[...].astype(F32)
    real = padded(both[:, 0, :])
    imag = padded(both[:, 1, :])
    by_real = jnp.concatenate([real, imag], axis=0).astype(BF16)
    by_imag = jnp.concatenate([-imag, real], axis=0).astype(BF16)
    copies[1].wait()
    copies[2].wait()
    fore = -forward[...].astype(F32)
    back = -backward[...].astype(F32)
    copies[3].wait()
    source = jnp.dot(by_real, pivot[0], preferred_element_type=F32)
    copies[4].wait()
    source = source + jnp.dot(by_imag, pivot[1], preferred_element_type=F32)
    for d in range(LAST):
        t, i = divmod(d, FIVE)
        lanes = slice(LANES * t, LANES * (t + 1))
        pieces = [source[at : at + n, lanes] for at, n, _ in placed(DEEP * i, DEEP)]
        out[d] = jnp.concatenate(pieces + [fore[:, lanes], back[:, lanes]], axis=0)
    tiles = [slice(LANES * t, LANES * (t + 1)) for t in range(TILES)]
    last = HALF + HEAD
    pieces = [source[last - TAIL : last, lanes] for lanes in tiles]
    pieces += [fore[:, lanes] for lanes in tiles] + [back[:, lanes] for lanes in tiles]
    pieces += [jnp.zeros((16 - TILES * (TAIL + 2), LANES), F32)]
    out[LAST] = jnp.concatenate(pieces, axis=0)


def placed(start, count):
    if start >= HEAD:
        return [(start + PAD, count, 0)]
    ahead = min(count, HEAD - start)
    rest = [(HALF, count - ahead, ahead)] if ahead < count else []
    return [(start, ahead, 0)] + rest


def is_last():
    return lax.axis_index("hull") % GROUP == NEAR[LAST]


def spread(block, row, first, last):
    whole = jnp.broadcast_to(block[row : row + 1], (16, LANES))
    parts = [jnp.broadcast_to(block[first + t : first + t + 1], (TAIL, LANES)) for t in range(TILES)]
    parts.append(jnp.zeros((16 - TILES * TAIL, LANES), F32))
    return jnp.where(last, jnp.concatenate(parts, axis=0), whole)


def by_tile(matrix):
    return [matrix[TAIL * t : TAIL * t + 1] for t in range(TILES)]


def reduce_body(shares, out):
    last = is_last()
    got = [shares[NEAR.index(j)] for j in range(GROUP)]
    fores = [spread(block, DEEP, TILES * TAIL, last) for block in got]
    backs = [spread(block, DEEP + 1, TILES * TAIL + TILES, last) for block in got]
    front, gain = got[0], fores[0]
    fronts, gains = [front], [gain]
    for j in range(1, GROUP):
        front = got[j] + front * fores[j]
        gain = gain * fores[j]
        fronts.append(front)
        gains.append(gain)
    motion, through, back_gain = front, gain, backs[GROUP - 1]
    for j in range(GROUP - 2, -1, -1):
        motion = fronts[j] + motion * backs[j]
        through = gains[j] + through * backs[j]
        back_gain = back_gain * backs[j]

    def pack(third):
        whole = [front[0:DEEP], motion[0:DEEP], gain[0:1], third[0:1], back_gain[0:1]]
        whole.append(jnp.zeros((1, LANES), F32))
        some = TILES * TAIL
        parts = [front[0:some]] + by_tile(gain) + by_tile(third)
        parts += [jnp.zeros((DEEP - some - 2 * TILES, LANES), F32), motion[0:some]] + by_tile(back_gain)
        parts.append(jnp.zeros((ENDS - DEEP - some - TILES, LANES), F32))
        return jnp.where(last, jnp.concatenate(parts, axis=0), jnp.concatenate(whole, axis=0))

    ahead, aft = pack(backs[GROUP - 1]), pack(through)
    mine = lax.axis_index("hull") // GROUP
    for place in range(SPAN):
        out[place] = jnp.where(mine < FAR[place], ahead, aft)


def solve_body(shares, reached, recovery, hotspots, frequency, spectrum, out, into, beyond, before):
    mine = lax.axis_index("hull") // GROUP
    last = is_last()
    some = TILES * TAIL
    zero = jnp.zeros((16, LANES), F32)
    ends = [reached[FAR.index(g)] for g in range(SPAN)]
    thirds = [spread(block, 2 * DEEP + 1, some + TILES, last) for block in ends]
    into[0] = zero
    before[0] = zero
    arriving = [zero]
    for g in range(SPAN - 1):
        arriving.append(ends[g][0:16] + arriving[g] * spread(ends[g], 2 * DEEP, some, last))
        into[g + 1] = arriving[g + 1]
        before[g + 1] = thirds[g]
    returning = zero
    beyond[SPAN - 1] = zero
    for g in range(SPAN - 1, 0, -1):
        returning = (
            ends[g][DEEP : DEEP + 16]
            + arriving[g] * thirds[g]
            + returning * spread(ends[g], 2 * DEEP + 2, DEEP + some, last)
        )
        beyond[g - 1] = returning
    enter = into[mine]
    front = enter
    got = [shares[NEAR.index(j)] for j in range(GROUP)]
    fronts = []
    for j in range(GROUP):
        front = got[j] + front * spread(got[j], DEEP, some, last)
        fronts.append(front)
    motion = beyond[mine]
    motions = [None] * GROUP
    for j in range(GROUP - 1, -1, -1):
        motion = fronts[j] + motion * spread(got[j], DEEP + 1, some + TILES, last)
        motions[j] = motion
    previous = enter + motion * before[mine]
    rest = jnp.zeros((32 - 2 * DEEP, LANES), F32)
    for j in range(GROUP):
        pieces = [motions[j][0:DEEP], previous[0:DEEP], rest]
        out[BACK.index(j)] = jnp.concatenate(pieces, axis=0)
        previous = motions[j]


def split(values, parts):
    pieces = []
    for _ in range(parts):
        piece = values.astype(BF16)
        values = values - piece.astype(F32)
        pieces.append(piece)
    return jnp.concatenate(pieces, axis=0)


def stress_body(got, recovery, hotspots, frequency, spectrum, motion_out, out, motion, stern):
    for part in range(2):
        rows = slice(HALF * part + HEAD, HALF * (part + 1))
        motion[rows] = jnp.zeros((PAD, MODES), F32)
        stern[rows] = jnp.zeros((PAD, MODES), F32)
    for place in range(GROUP):
        d = NEAR.index(BACK[place])
        t, i = divmod(d, FIVE)
        pieces = [(t, at, n, skip) for at, n, skip in placed(DEEP * i, DEEP)]
        if d == LAST:
            pieces = [(t, HALF + HEAD - TAIL, TAIL, TAIL * t) for t in range(TILES)]
        for t, at, n, skip in pieces:
            lanes = slice(LANES * t, LANES * (t + 1))
            motion[at : at + n, lanes] = got[place, skip : skip + n]
            stern[at : at + n, lanes] = got[place, DEEP + skip : DEEP + skip + n]
    motion_out[0, 0, :, 0, :] = motion[0:HEAD]
    motion_out[0, 0, :, 1, :] = motion[HALF : HALF + HEAD]
    contract = (((1,), (1,)), ((), ()))
    both = lax.dot_general(
        split(stern[...], 2), recovery[0, :, 0:MODES], contract, preferred_element_type=F32
    ) + lax.dot_general(
        split(motion[...], 2), recovery[0, :, MODES:], contract, preferred_element_type=F32
    )
    stress = both[0 : 2 * HALF] + both[2 * HALF :]
    power = stress[0:HALF] ** 2 + stress[HALF:] ** 2
    rows = lax.broadcasted_iota(jnp.int32, (HALF, HEAD), 0)
    columns = lax.broadcasted_iota(jnp.int32, (HALF, HEAD), 1)
    weight = jnp.sum(jnp.where(rows == columns, spectrum[...], 0.0), axis=1, keepdims=True)
    energy = power * (weight * (1.2 / 4))
    elements = lax.broadcasted_iota(jnp.int32, (POINTS, POINTS), 0)
    chosen = jnp.where(elements == hotspots[...], 1.0, 0.0).astype(BF16)
    thirds = jnp.dot(split(energy, 3), chosen, preferred_element_type=F32)
    energy = thirds[0:HALF] + (thirds[HALF : 2 * HALF] + thirds[2 * HALF :])
    here = jnp.broadcast_to(frequency[...].reshape(1, 1), (1, POINTS))
    rows = lax.broadcasted_iota(jnp.int32, (HALF, POINTS), 0)
    packed = jnp.where(rows < HEAD, energy, here)
    for f in range(4):
        out[f] = packed


def damage_body(got, moments_out, damage_out):
    zeroth = jnp.zeros((HEAD, POINTS), F32)
    second = zeroth
    fourth = zeroth
    for f in range(4):
        energy = got[f, 0:HEAD]
        square = got[f, HEAD : HEAD + 1] ** 2
        zeroth = zeroth + energy
        second = second + energy * square
        fourth = fourth + energy * (square * square)
    moments_out[0, :, 0, :] = zeroth
    moments_out[1, :, 0, :] = second
    moments_out[2, :, 0, :] = fourth
    damage_out[:, 0, :] = (
        0.5 * jnp.log(fourth / second)
        + 1.5 * jnp.log(zeroth)
        + jnp.log(0.5 + 0.5 * second / jnp.sqrt(zeroth * fourth))
    )


def exchange(values, axis, groups):
    return lax.all_to_all(values, axis, 0, 0, axis_index_groups=groups, tiled=True)


def per_device(wave_loads, pivot_inverse, forward, backward, recovery, hotspots, frequency, spectrum):
    near = [[GROUP * g + j for j in NEAR] for g in range(SPAN)]
    back = [[GROUP * g + j for j in BACK] for g in range(SPAN)]
    far = [[GROUP * g + j for g in FAR] for j in range(GROUP)]
    (source,) = call(
        source_body,
        [(GROUP, 16, LANES)],
        jnp.transpose(wave_loads, (0, 1, 3, 2, 4)),
        pivot_inverse,
        forward[0],
        backward[0],
        spaces=[pl.ANY] * 4,
        vmem_mib=56,
        scratch=[
            pltpu.VMEM((HEAD, 2, MODES), BF16),
            pltpu.VMEM((2, MODES, MODES), BF16),
            pltpu.VMEM((1, MODES), BF16),
            pltpu.VMEM((1, MODES), BF16),
            pltpu.SemaphoreType.DMA((5,)),
        ],
    )
    shares = exchange(source, "hull", near)
    (ends,) = call(reduce_body, [(SPAN, ENDS, LANES)], shares)
    ends = exchange(ends, "hull", far)
    (solved,) = call(
        solve_body,
        [(GROUP, 32, LANES)],
        shares,
        ends,
        recovery,
        hotspots,
        frequency,
        spectrum,
        scratch=[pltpu.VMEM((SPAN, 16, LANES), F32)] * 3,
    )
    solved = exchange(solved, "hull", back)
    motion, energy = call(
        stress_body,
        [(1, 1, HEAD, 2, MODES), (4, HALF, POINTS)],
        solved,
        recovery,
        hotspots,
        frequency,
        spectrum,
        scratch=[pltpu.VMEM((2 * HALF, MODES), F32)] * 2,
    )
    energy = exchange(energy, "freq", [WAVES])
    moments, damage = call(damage_body, [(3, HEAD, 1, POINTS), (HEAD, 1, POINTS)], energy)
    return (
        jnp.transpose(motion, (0, 1, 3, 2, 4)),
        jnp.transpose(moments, (0, 2, 1, 3)),
        jnp.transpose(damage, (1, 0, 2)),
    )


def solution(mesh):
    in_specs = (
        P("freq", "hull", None, None, None),
        P("freq", "hull", None, None, None),
        P("freq", "hull", None),
        P("freq", "hull", None),
        P("hull", None, None),
        P("hull", None),
        P("freq"),
        P("freq", None),
    )
    out_specs = (
        P("freq", "hull", None, None, None),
        P(None, "hull", None, None),
        P("hull", None, None),
    )
    return jax.shard_map(per_device, mesh=mesh, in_specs=in_specs, out_specs=out_specs, check_vma=False)
```

```python
import jax
import jax.numpy as jnp
from jax import lax
from jax.experimental import pallas as pl
from jax.experimental.pallas import tpu as pltpu
from jax.sharding import PartitionSpec as P

SPAN, GROUP = 8, 16
HEAD, MODES, POINTS = 36, 384, 256
LANES = 128
TILES = MODES // LANES
HALF = 40
PAD = HALF - HEAD
DEEP, FIVE = 14, 5
TAIL = 2 * HEAD - DEEP * FIVE
LAST = FIVE * TILES
ENDS = 32
NEAR = (15, 14, 13, 12, 11, 10, 9, 8, 7, 6, 5, 4, 3, 2, 1, 0)
BACK = (4, 5, 6, 7, 8, 9, 10, 11, 12, 13, 14, 15, 0, 1, 2, 3)
FAR = (5, 0, 1, 2, 3, 4, 6, 7)
WAVES = (2, 3, 1, 0)
F32 = jnp.float32
BF16 = jnp.bfloat16


def call(body, shapes, *args, spaces=None, out_spaces=None, vmem_mib=12, scratch=()):
    outs = [jax.ShapeDtypeStruct(shape, F32) for shape in shapes]
    spaces = spaces or [pltpu.VMEM] * len(args)
    out_spaces = out_spaces or [pltpu.VMEM] * len(outs)
    return pl.pallas_call(
        body,
        out_shape=outs,
        in_specs=[pl.BlockSpec(memory_space=space) for space in spaces],
        out_specs=[pl.BlockSpec(memory_space=space) for space in out_spaces],
        scratch_shapes=list(scratch),
        compiler_params=pltpu.CompilerParams(vmem_limit_bytes=vmem_mib * 2**20),
    )(*args)


def padded(rows):
    return jnp.concatenate([rows, jnp.zeros((HALF - HEAD, rows.shape[1]), rows.dtype)], axis=0)


def source_body(loads_hbm, pivot_hbm, forward_hbm, backward_hbm, out, loads, pivot, forward, backward, arrived):
    copies = [
        pltpu.make_async_copy(loads_hbm.at[0, 0], loads, arrived.at[0]),
        pltpu.make_async_copy(forward_hbm, forward, arrived.at[1]),
        pltpu.make_async_copy(backward_hbm, backward, arrived.at[2]),
        pltpu.make_async_copy(pivot_hbm.at[0, 0, 0], pivot.at[0], arrived.at[3]),
        pltpu.make_async_copy(pivot_hbm.at[0, 0, 1], pivot.at[1], arrived.at[4]),
    ]
    for copy in copies:
        copy.start()
    copies[0].wait()
    both = loads[...].astype(F32)
    real = padded(both[:, 0, :])
    imag = padded(both[:, 1, :])
    by_real = jnp.concatenate([real, imag], axis=0).astype(BF16)
    by_imag = jnp.concatenate([-imag, real], axis=0).astype(BF16)
    copies[1].wait()
    copies[2].wait()
    fore = -forward[...].astype(F32)
    back = -backward[...].astype(F32)
    copies[3].wait()
    source = jnp.dot(by_real, pivot[0], preferred_element_type=F32)
    copies[4].wait()
    source = source + jnp.dot(by_imag, pivot[1], preferred_element_type=F32)
    for d in range(LAST):
        t, i = divmod(d, FIVE)
        lanes = slice(LANES * t, LANES * (t + 1))
        pieces = [source[at : at + n, lanes] for at, n, _ in placed(DEEP * i, DEEP)]
        out[d] = jnp.concatenate(pieces + [fore[:, lanes], back[:, lanes]], axis=0)
    tiles = [slice(LANES * t, LANES * (t + 1)) for t in range(TILES)]
    last = HALF + HEAD
    pieces = [source[last - TAIL : last, lanes] for lanes in tiles]
    pieces += [fore[:, lanes] for lanes in tiles] + [back[:, lanes] for lanes in tiles]
    pieces += [jnp.zeros((16 - TILES * (TAIL + 2), LANES), F32)]
    out[LAST] = jnp.concatenate(pieces, axis=0)


def placed(start, count):
    if start >= HEAD:
        return [(start + PAD, count, 0)]
    ahead = min(count, HEAD - start)
    rest = [(HALF, count - ahead, ahead)] if ahead < count else []
    return [(start, ahead, 0)] + rest


def is_last():
    return lax.axis_index("hull") % GROUP == NEAR[LAST]


def spread(block, row, first, last):
    whole = jnp.broadcast_to(block[row : row + 1], (16, LANES))
    parts = [jnp.broadcast_to(block[first + t : first + t + 1], (TAIL, LANES)) for t in range(TILES)]
    parts.append(jnp.zeros((16 - TILES * TAIL, LANES), F32))
    return jnp.where(last, jnp.concatenate(parts, axis=0), whole)


def by_tile(matrix):
    return [matrix[TAIL * t : TAIL * t + 1] for t in range(TILES)]


def reduce_body(shares, recovery, hotspots, frequency, spectrum, out):
    last = is_last()
    got = [shares[NEAR.index(j)] for j in range(GROUP)]
    fores = [spread(block, DEEP, TILES * TAIL, last) for block in got]
    backs = [spread(block, DEEP + 1, TILES * TAIL + TILES, last) for block in got]
    front, gain = got[0], fores[0]
    fronts, gains = [front], [gain]
    for j in range(1, GROUP):
        front = got[j] + front * fores[j]
        gain = gain * fores[j]
        fronts.append(front)
        gains.append(gain)
    motion, through, back_gain = front, gain, backs[GROUP - 1]
    for j in range(GROUP - 2, -1, -1):
        motion = fronts[j] + motion * backs[j]
        through = gains[j] + through * backs[j]
        back_gain = back_gain * backs[j]

    def pack(third):
        whole = [front[0:DEEP], motion[0:DEEP], gain[0:1], third[0:1], back_gain[0:1]]
        whole.append(jnp.zeros((1, LANES), F32))
        some = TILES * TAIL
        parts = [front[0:some]] + by_tile(gain) + by_tile(third)
        parts += [jnp.zeros((DEEP - some - 2 * TILES, LANES), F32), motion[0:some]] + by_tile(back_gain)
        parts.append(jnp.zeros((ENDS - DEEP - some - TILES, LANES), F32))
        return jnp.where(last, jnp.concatenate(parts, axis=0), jnp.concatenate(whole, axis=0))

    ahead, aft = pack(backs[GROUP - 1]), pack(through)
    mine = lax.axis_index("hull") // GROUP
    for place in range(SPAN):
        out[place] = jnp.where(mine < FAR[place], ahead, aft)


def solve_body(shares, reached, out, into, beyond, before):
    mine = lax.axis_index("hull") // GROUP
    last = is_last()
    some = TILES * TAIL
    zero = jnp.zeros((16, LANES), F32)
    ends = [reached[FAR.index(g)] for g in range(SPAN)]
    thirds = [spread(block, 2 * DEEP + 1, some + TILES, last) for block in ends]
    into[0] = zero
    before[0] = zero
    arriving = [zero]
    for g in range(SPAN - 1):
        arriving.append(ends[g][0:16] + arriving[g] * spread(ends[g], 2 * DEEP, some, last))
        into[g + 1] = arriving[g + 1]
        before[g + 1] = thirds[g]
    returning = zero
    beyond[SPAN - 1] = zero
    for g in range(SPAN - 1, 0, -1):
        returning = (
            ends[g][DEEP : DEEP + 16]
            + arriving[g] * thirds[g]
            + returning * spread(ends[g], 2 * DEEP + 2, DEEP + some, last)
        )
        beyond[g - 1] = returning
    enter = into[mine]
    front = enter
    got = [shares[NEAR.index(j)] for j in range(GROUP)]
    fronts = []
    for j in range(GROUP):
        front = got[j] + front * spread(got[j], DEEP, some, last)
        fronts.append(front)
    motion = beyond[mine]
    motions = [None] * GROUP
    for j in range(GROUP - 1, -1, -1):
        motion = fronts[j] + motion * spread(got[j], DEEP + 1, some + TILES, last)
        motions[j] = motion
    previous = enter + motion * before[mine]
    rest = jnp.zeros((32 - 2 * DEEP, LANES), F32)
    for j in range(GROUP):
        pieces = [motions[j][0:DEEP], previous[0:DEEP], rest]
        out[BACK.index(j)] = jnp.concatenate(pieces, axis=0)
        previous = motions[j]


def split(values, parts):
    pieces = []
    for _ in range(parts):
        piece = values.astype(BF16)
        values = values - piece.astype(F32)
        pieces.append(piece)
    return jnp.concatenate(pieces, axis=0)


def stress_body(got, recovery, hotspots, frequency, spectrum, motion_out, out, motion, stern):
    for part in range(2):
        rows = slice(HALF * part + HEAD, HALF * (part + 1))
        motion[rows] = jnp.zeros((PAD, MODES), F32)
        stern[rows] = jnp.zeros((PAD, MODES), F32)
    for place in range(GROUP):
        d = NEAR.index(BACK[place])
        t, i = divmod(d, FIVE)
        pieces = [(t, at, n, skip) for at, n, skip in placed(DEEP * i, DEEP)]
        if d == LAST:
            pieces = [(t, HALF + HEAD - TAIL, TAIL, TAIL * t) for t in range(TILES)]
        for t, at, n, skip in pieces:
            lanes = slice(LANES * t, LANES * (t + 1))
            motion[at : at + n, lanes] = got[place, skip : skip + n]
            stern[at : at + n, lanes] = got[place, DEEP + skip : DEEP + skip + n]
    motion_out[0, 0, :, 0, :] = motion[0:HEAD]
    motion_out[0, 0, :, 1, :] = motion[HALF : HALF + HEAD]
    contract = (((1,), (1,)), ((), ()))
    both = lax.dot_general(
        split(stern[...], 2), recovery[0, :, 0:MODES], contract, preferred_element_type=F32
    ) + lax.dot_general(
        split(motion[...], 2), recovery[0, :, MODES:], contract, preferred_element_type=F32
    )
    stress = both[0 : 2 * HALF] + both[2 * HALF :]
    power = stress[0:HALF] ** 2 + stress[HALF:] ** 2
    rows = lax.broadcasted_iota(jnp.int32, (HALF, HEAD), 0)
    columns = lax.broadcasted_iota(jnp.int32, (HALF, HEAD), 1)
    weight = jnp.sum(jnp.where(rows == columns, spectrum[...], 0.0), axis=1, keepdims=True)
    energy = power * (weight * (1.2 / 4))
    elements = lax.broadcasted_iota(jnp.int32, (POINTS, POINTS), 0)
    chosen = jnp.where(elements == hotspots[...], 1.0, 0.0).astype(BF16)
    thirds = jnp.dot(split(energy, 3), chosen, preferred_element_type=F32)
    energy = thirds[0:HALF] + (thirds[HALF : 2 * HALF] + thirds[2 * HALF :])
    here = jnp.broadcast_to(frequency[...].reshape(1, 1), (1, POINTS))
    rows = lax.broadcasted_iota(jnp.int32, (HALF, POINTS), 0)
    packed = jnp.where(rows < HEAD, energy, here)
    for f in range(4):
        out[f] = packed


def damage_body(got, moments_out, damage_out):
    zeroth = jnp.zeros((HEAD, POINTS), F32)
    second = zeroth
    fourth = zeroth
    for f in range(4):
        energy = got[f, 0:HEAD]
        square = got[f, HEAD : HEAD + 1] ** 2
        zeroth = zeroth + energy
        second = second + energy * square
        fourth = fourth + energy * (square * square)
    moments_out[0, :, 0, :] = zeroth
    moments_out[1, :, 0, :] = second
    moments_out[2, :, 0, :] = fourth
    damage_out[:, 0, :] = (
        0.5 * jnp.log(fourth / second)
        + 1.5 * jnp.log(zeroth)
        + jnp.log(0.5 + 0.5 * second / jnp.sqrt(zeroth * fourth))
    )


def exchange(values, axis, groups):
    return lax.all_to_all(values, axis, 0, 0, axis_index_groups=groups, tiled=True)


def per_device(wave_loads, pivot_inverse, forward, backward, recovery, hotspots, frequency, spectrum):
    near = [[GROUP * g + j for j in NEAR] for g in range(SPAN)]
    back = [[GROUP * g + j for j in BACK] for g in range(SPAN)]
    far = [[GROUP * g + j for g in FAR] for j in range(GROUP)]
    (source,) = call(
        source_body,
        [(GROUP, 16, LANES)],
        jnp.transpose(wave_loads, (0, 1, 3, 2, 4)),
        pivot_inverse,
        forward[0],
        backward[0],
        spaces=[pl.ANY] * 4,
        vmem_mib=56,
        scratch=[
            pltpu.VMEM((HEAD, 2, MODES), BF16),
            pltpu.VMEM((2, MODES, MODES), BF16),
            pltpu.VMEM((1, MODES), BF16),
            pltpu.VMEM((1, MODES), BF16),
            pltpu.SemaphoreType.DMA((5,)),
        ],
    )
    shares = exchange(source, "hull", near)
    (ends,) = call(reduce_body, [(SPAN, ENDS, LANES)], shares, recovery, hotspots, frequency, spectrum)
    ends = exchange(ends, "hull", far)
    (solved,) = call(
        solve_body,
        [(GROUP, 32, LANES)],
        shares,
        ends,
        scratch=[pltpu.VMEM((SPAN, 16, LANES), F32)] * 3,
    )
    solved = exchange(solved, "hull", back)
    motion, energy = call(
        stress_body,
        [(1, 1, HEAD, 2, MODES), (4, HALF, POINTS)],
        solved,
        recovery,
        hotspots,
        frequency,
        spectrum,
        scratch=[pltpu.VMEM((2 * HALF, MODES), F32)] * 2,
    )
    energy = exchange(energy, "freq", [WAVES])
    moments, damage = call(damage_body, [(3, HEAD, 1, POINTS), (HEAD, 1, POINTS)], energy)
    return (
        jnp.transpose(motion, (0, 1, 3, 2, 4)),
        jnp.transpose(moments, (0, 2, 1, 3)),
        jnp.transpose(damage, (1, 0, 2)),
    )


def solution(mesh):
    in_specs = (
        P("freq", "hull", None, None, None),
        P("freq", "hull", None, None, None),
        P("freq", "hull", None),
        P("freq", "hull", None),
        P("hull", None, None),
        P("hull", None),
        P("freq"),
        P("freq", None),
    )
    out_specs = (
        P("freq", "hull", None, None, None),
        P(None, "hull", None, None),
        P("hull", None, None),
    )
    return jax.shard_map(per_device, mesh=mesh, in_specs=in_specs, out_specs=out_specs, check_vma=False)
```

```python
import jax
import jax.numpy as jnp
from jax import lax
from jax.experimental import pallas as pl
from jax.experimental.pallas import tpu as pltpu
from jax.sharding import PartitionSpec as P

SPAN, GROUP = 8, 16
HEAD, MODES, POINTS = 36, 384, 256
LANES = 128
TILES = MODES // LANES
HALF = 40
PAD = HALF - HEAD
DEEP, FIVE = 14, 5
TAIL = 2 * HEAD - DEEP * FIVE
LAST = FIVE * TILES
ENDS = 32
NEAR = (15, 14, 13, 12, 11, 10, 9, 8, 7, 6, 5, 4, 3, 2, 1, 0)
BACK = (4, 5, 6, 7, 8, 9, 10, 11, 12, 13, 14, 15, 0, 1, 2, 3)
FAR = (5, 0, 1, 2, 3, 4, 6, 7)
WAVES = (2, 3, 1, 0)
F32 = jnp.float32
BF16 = jnp.bfloat16


def call(body, shapes, *args, kind=F32, spaces=None, out_spaces=None, vmem_mib=12, scratch=()):
    outs = [jax.ShapeDtypeStruct(shape, kind) for shape in shapes]
    spaces = spaces or [pltpu.VMEM] * len(args)
    out_spaces = out_spaces or [pltpu.VMEM] * len(outs)
    return pl.pallas_call(
        body,
        out_shape=outs,
        in_specs=[pl.BlockSpec(memory_space=space) for space in spaces],
        out_specs=[pl.BlockSpec(memory_space=space) for space in out_spaces],
        scratch_shapes=list(scratch),
        compiler_params=pltpu.CompilerParams(vmem_limit_bytes=vmem_mib * 2**20),
    )(*args)


def padded(rows):
    return jnp.concatenate([rows, jnp.zeros((HALF - HEAD, rows.shape[1]), rows.dtype)], axis=0)


def source_body(loads_hbm, pivot_hbm, forward_hbm, backward_hbm, out, loads, pivot, forward, backward, arrived):
    copies = [
        pltpu.make_async_copy(loads_hbm.at[0, 0], loads, arrived.at[0]),
        pltpu.make_async_copy(forward_hbm, forward, arrived.at[1]),
        pltpu.make_async_copy(backward_hbm, backward, arrived.at[2]),
        pltpu.make_async_copy(pivot_hbm.at[0, 0, 0], pivot.at[0], arrived.at[3]),
        pltpu.make_async_copy(pivot_hbm.at[0, 0, 1], pivot.at[1], arrived.at[4]),
    ]
    for i in (3, 0, 4, 1, 2):
        copies[i].start()
    copies[0].wait()
    both = loads[...].astype(F32)
    real = padded(both[:, 0, :])
    imag = padded(both[:, 1, :])
    by_real = jnp.concatenate([real, imag], axis=0).astype(BF16)
    by_imag = jnp.concatenate([-imag, real], axis=0).astype(BF16)
    copies[1].wait()
    copies[2].wait()
    fore = -forward[...].astype(F32)
    back = -backward[...].astype(F32)
    copies[3].wait()
    source = jnp.dot(by_real, pivot[0], preferred_element_type=F32)
    copies[4].wait()
    source = source + jnp.dot(by_imag, pivot[1], preferred_element_type=F32)
    for d in range(LAST):
        t, i = divmod(d, FIVE)
        lanes = slice(LANES * t, LANES * (t + 1))
        pieces = [source[at : at + n, lanes] for at, n, _ in placed(DEEP * i, DEEP)]
        out[d] = jnp.concatenate(pieces + [fore[:, lanes], back[:, lanes]], axis=0)
    tiles = [slice(LANES * t, LANES * (t + 1)) for t in range(TILES)]
    last = HALF + HEAD
    pieces = [source[last - TAIL : last, lanes] for lanes in tiles]
    pieces += [fore[:, lanes] for lanes in tiles] + [back[:, lanes] for lanes in tiles]
    pieces += [jnp.zeros((16 - TILES * (TAIL + 2), LANES), F32)]
    out[LAST] = jnp.concatenate(pieces, axis=0)


def placed(start, count):
    if start >= HEAD:
        return [(start + PAD, count, 0)]
    ahead = min(count, HEAD - start)
    rest = [(HALF, count - ahead, ahead)] if ahead < count else []
    return [(start, ahead, 0)] + rest


def is_last():
    return lax.axis_index("hull") % GROUP == NEAR[LAST]


def spread(block, row, first, last):
    whole = jnp.broadcast_to(block[row : row + 1], (16, LANES))
    parts = [jnp.broadcast_to(block[first + t : first + t + 1], (TAIL, LANES)) for t in range(TILES)]
    parts.append(jnp.zeros((16 - TILES * TAIL, LANES), F32))
    return jnp.where(last, jnp.concatenate(parts, axis=0), whole)


def by_tile(matrix):
    return [matrix[TAIL * t : TAIL * t + 1] for t in range(TILES)]


def reduce_body(shares, picked, frequency, spectrum, out):
    last = is_last()
    got = [shares[NEAR.index(j)] for j in range(GROUP)]
    fores = [spread(block, DEEP, TILES * TAIL, last) for block in got]
    backs = [spread(block, DEEP + 1, TILES * TAIL + TILES, last) for block in got]
    front, gain = got[0], fores[0]
    fronts, gains = [front], [gain]
    for j in range(1, GROUP):
        front = got[j] + front * fores[j]
        gain = gain * fores[j]
        fronts.append(front)
        gains.append(gain)
    motion, through, back_gain = front, gain, backs[GROUP - 1]
    for j in range(GROUP - 2, -1, -1):
        motion = fronts[j] + motion * backs[j]
        through = gains[j] + through * backs[j]
        back_gain = back_gain * backs[j]

    def pack(third):
        whole = [front[0:DEEP], motion[0:DEEP], gain[0:1], third[0:1], back_gain[0:1]]
        whole.append(jnp.zeros((1, LANES), F32))
        some = TILES * TAIL
        parts = [front[0:some]] + by_tile(gain) + by_tile(third)
        parts += [jnp.zeros((DEEP - some - 2 * TILES, LANES), F32), motion[0:some]] + by_tile(back_gain)
        parts.append(jnp.zeros((ENDS - DEEP - some - TILES, LANES), F32))
        return jnp.where(last, jnp.concatenate(parts, axis=0), jnp.concatenate(whole, axis=0))

    ahead, aft = pack(backs[GROUP - 1]), pack(through)
    mine = lax.axis_index("hull") // GROUP
    for place in range(SPAN):
        out[place] = jnp.where(mine < FAR[place], ahead, aft)


def solve_body(shares, reached, out, into, beyond, before):
    mine = lax.axis_index("hull") // GROUP
    last = is_last()
    some = TILES * TAIL
    zero = jnp.zeros((16, LANES), F32)
    ends = [reached[FAR.index(g)] for g in range(SPAN)]
    thirds = [spread(block, 2 * DEEP + 1, some + TILES, last) for block in ends]
    into[0] = zero
    before[0] = zero
    arriving = [zero]
    for g in range(SPAN - 1):
        arriving.append(ends[g][0:16] + arriving[g] * spread(ends[g], 2 * DEEP, some, last))
        into[g + 1] = arriving[g + 1]
        before[g + 1] = thirds[g]
    returning = zero
    beyond[SPAN - 1] = zero
    for g in range(SPAN - 1, 0, -1):
        returning = (
            ends[g][DEEP : DEEP + 16]
            + arriving[g] * thirds[g]
            + returning * spread(ends[g], 2 * DEEP + 2, DEEP + some, last)
        )
        beyond[g - 1] = returning
    enter = into[mine]
    front = enter
    got = [shares[NEAR.index(j)] for j in range(GROUP)]
    fronts = []
    for j in range(GROUP):
        front = got[j] + front * spread(got[j], DEEP, some, last)
        fronts.append(front)
    motion = beyond[mine]
    motions = [None] * GROUP
    for j in range(GROUP - 1, -1, -1):
        motion = fronts[j] + motion * spread(got[j], DEEP + 1, some + TILES, last)
        motions[j] = motion
    previous = enter + motion * before[mine]
    for j in range(GROUP):
        both = jnp.concatenate([motions[j][0:DEEP], previous[0:DEEP]], axis=0)
        for q in range(2 * DEEP // 4):
            out[BACK.index(j), q] = both[4 * q : 4 * q + 4]
        previous = motions[j]


def split(values, parts):
    pieces = []
    for _ in range(parts):
        piece = values.astype(BF16)
        values = values - piece.astype(F32)
        pieces.append(piece)
    return jnp.concatenate(pieces, axis=0)


def pick_body(recovery, hotspots, picked):
    elements = lax.broadcasted_iota(jnp.int32, (POINTS, POINTS), 0)
    chosen = jnp.where(elements == hotspots[...], 1.0, 0.0).astype(BF16)
    contract = (((0,), (0,)), ((), ()))
    rows = lax.dot_general(chosen, recovery[0], contract, preferred_element_type=F32)
    picked[...] = rows.astype(BF16)


def stress_body(got, picked, frequency, spectrum, motion_out, out, motion, stern):
    for part in range(2):
        rows = slice(HALF * part + HEAD, HALF * (part + 1))
        motion[rows] = jnp.zeros((PAD, MODES), F32)
        stern[rows] = jnp.zeros((PAD, MODES), F32)
    for place in range(GROUP):
        d = NEAR.index(BACK[place])
        block = jnp.concatenate([got[place, q] for q in range(2 * DEEP // 4)], axis=0)
        t, i = divmod(d, FIVE)
        pieces = [(t, at, n, skip) for at, n, skip in placed(DEEP * i, DEEP)]
        if d == LAST:
            pieces = [(t, HALF + HEAD - TAIL, TAIL, TAIL * t) for t in range(TILES)]
        for t, at, n, skip in pieces:
            lanes = slice(LANES * t, LANES * (t + 1))
            motion[at : at + n, lanes] = block[skip : skip + n]
            stern[at : at + n, lanes] = block[DEEP + skip : DEEP + skip + n]
    motion_out[0, 0, :, 0, :] = motion[0:HEAD]
    motion_out[0, 0, :, 1, :] = motion[HALF : HALF + HEAD]
    contract = (((1,), (1,)), ((), ()))
    both = lax.dot_general(
        split(stern[...], 2), picked[:, 0:MODES], contract, preferred_element_type=F32
    ) + lax.dot_general(
        split(motion[...], 2), picked[:, MODES:], contract, preferred_element_type=F32
    )
    stress = both[0 : 2 * HALF] + both[2 * HALF :]
    power = stress[0:HALF] ** 2 + stress[HALF:] ** 2
    rows = lax.broadcasted_iota(jnp.int32, (HALF, HEAD), 0)
    columns = lax.broadcasted_iota(jnp.int32, (HALF, HEAD), 1)
    weight = jnp.sum(jnp.where(rows == columns, spectrum[...], 0.0), axis=1, keepdims=True)
    energy = power * (weight * (1.2 / 4))
    here = jnp.broadcast_to(frequency[...].reshape(1, 1), (1, POINTS))
    rows = lax.broadcasted_iota(jnp.int32, (HALF, POINTS), 0)
    packed = jnp.where(rows < HEAD, energy, here)
    for f in range(4):
        out[f] = packed


def damage_body(got, moments_out, damage_out):
    zeroth = jnp.zeros((HEAD, POINTS), F32)
    second = zeroth
    fourth = zeroth
    for f in range(4):
        energy = got[f, 0:HEAD]
        square = got[f, HEAD : HEAD + 1] ** 2
        zeroth = zeroth + energy
        second = second + energy * square
        fourth = fourth + energy * (square * square)
    moments_out[0, :, 0, :] = zeroth
    moments_out[1, :, 0, :] = second
    moments_out[2, :, 0, :] = fourth
    damage_out[:, 0, :] = (
        0.5 * jnp.log(fourth / second)
        + 1.5 * jnp.log(zeroth)
        + jnp.log(0.5 + 0.5 * second / jnp.sqrt(zeroth * fourth))
    )


def exchange(values, axis, groups):
    return lax.all_to_all(values, axis, 0, 0, axis_index_groups=groups, tiled=True)


def per_device(wave_loads, pivot_inverse, forward, backward, recovery, hotspots, frequency, spectrum):
    near = [[GROUP * g + j for j in NEAR] for g in range(SPAN)]
    back = [[GROUP * g + j for j in BACK] for g in range(SPAN)]
    far = [[GROUP * g + j for g in FAR] for j in range(GROUP)]
    (source,) = call(
        source_body,
        [(GROUP, 16, LANES)],
        jnp.transpose(wave_loads, (0, 1, 3, 2, 4)),
        pivot_inverse,
        forward[0],
        backward[0],
        spaces=[pl.ANY] * 4,
        vmem_mib=56,
        scratch=[
            pltpu.VMEM((HEAD, 2, MODES), BF16),
            pltpu.VMEM((2, MODES, MODES), BF16),
            pltpu.VMEM((1, MODES), BF16),
            pltpu.VMEM((1, MODES), BF16),
            pltpu.SemaphoreType.DMA((5,)),
        ],
    )
    (picked,) = call(pick_body, [(POINTS, 2 * MODES)], recovery, hotspots, kind=BF16)
    shares = exchange(source, "hull", near)
    (ends,) = call(reduce_body, [(SPAN, ENDS, LANES)], shares, picked, frequency, spectrum)
    ends = exchange(ends, "hull", far)
    (solved,) = call(
        solve_body,
        [(GROUP, 2 * DEEP // 4, 4, LANES)],
        shares,
        ends,
        scratch=[pltpu.VMEM((SPAN, 16, LANES), F32)] * 3,
    )
    solved = exchange(solved, "hull", back)
    motion, energy = call(
        stress_body,
        [(1, 1, HEAD, 2, MODES), (4, HALF, POINTS)],
        solved,
        picked,
        frequency,
        spectrum,
        scratch=[pltpu.VMEM((2 * HALF, MODES), F32)] * 2,
    )
    energy = exchange(energy, "freq", [WAVES])
    moments, damage = call(damage_body, [(3, HEAD, 1, POINTS), (HEAD, 1, POINTS)], energy)
    return (
        jnp.transpose(motion, (0, 1, 3, 2, 4)),
        jnp.transpose(moments, (0, 2, 1, 3)),
        jnp.transpose(damage, (1, 0, 2)),
    )


def solution(mesh):
    in_specs = (
        P("freq", "hull", None, None, None),
        P("freq", "hull", None, None, None),
        P("freq", "hull", None),
        P("freq", "hull", None),
        P("hull", None, None),
        P("hull", None),
        P("freq"),
        P("freq", None),
    )
    out_specs = (
        P("freq", "hull", None, None, None),
        P(None, "hull", None, None),
        P("hull", None, None),
    )
    return jax.shard_map(per_device, mesh=mesh, in_specs=in_specs, out_specs=out_specs, check_vma=False)
```

```python
import jax
import jax.numpy as jnp
from jax import lax
from jax.experimental import pallas as pl
from jax.experimental.pallas import tpu as pltpu
from jax.sharding import PartitionSpec as P

SPAN, GROUP = 8, 16
HEAD, MODES, POINTS = 36, 384, 256
LANES = 128
TILES = MODES // LANES
HALF = 40
PAD = HALF - HEAD
DEEP, FIVE = 14, 5
TAIL = 2 * HEAD - DEEP * FIVE
LAST = FIVE * TILES
ENDS = 32
NEAR = (15, 14, 13, 12, 11, 10, 9, 8, 7, 6, 5, 4, 3, 2, 1, 0)
BACK = (4, 5, 6, 7, 8, 9, 10, 11, 12, 13, 14, 15, 0, 1, 2, 3)
FAR = (5, 0, 1, 2, 3, 4, 6, 7)
WAVES = (2, 3, 1, 0)
F32 = jnp.float32
BF16 = jnp.bfloat16


def call(body, shapes, *args, kind=F32, spaces=None, out_spaces=None, vmem_mib=12, scratch=()):
    outs = [jax.ShapeDtypeStruct(shape, kind) for shape in shapes]
    spaces = spaces or [pltpu.VMEM] * len(args)
    out_spaces = out_spaces or [pltpu.VMEM] * len(outs)
    return pl.pallas_call(
        body,
        out_shape=outs,
        in_specs=[pl.BlockSpec(memory_space=space) for space in spaces],
        out_specs=[pl.BlockSpec(memory_space=space) for space in out_spaces],
        scratch_shapes=list(scratch),
        compiler_params=pltpu.CompilerParams(vmem_limit_bytes=vmem_mib * 2**20),
    )(*args)


def padded(rows):
    return jnp.concatenate([rows, jnp.zeros((HALF - HEAD, rows.shape[1]), rows.dtype)], axis=0)


def source_body(loads_hbm, pivot_hbm, forward_hbm, backward_hbm, out, loads, pivot, forward, backward, arrived):
    copies = [
        pltpu.make_async_copy(loads_hbm.at[0, 0], loads, arrived.at[0]),
        pltpu.make_async_copy(forward_hbm, forward, arrived.at[1]),
        pltpu.make_async_copy(backward_hbm, backward, arrived.at[2]),
        pltpu.make_async_copy(pivot_hbm.at[0, 0, 0], pivot.at[0], arrived.at[3]),
        pltpu.make_async_copy(pivot_hbm.at[0, 0, 1], pivot.at[1], arrived.at[4]),
    ]
    for i in (3, 0, 4, 1, 2):
        copies[i].start()
    copies[0].wait()
    both = loads[...].astype(F32)
    real = padded(both[:, 0, :])
    imag = padded(both[:, 1, :])
    by_real = jnp.concatenate([real, imag], axis=0).astype(BF16)
    by_imag = jnp.concatenate([-imag, real], axis=0).astype(BF16)
    copies[1].wait()
    copies[2].wait()
    fore = -forward[...].astype(F32)
    back = -backward[...].astype(F32)
    copies[3].wait()
    source = jnp.dot(by_real, pivot[0], preferred_element_type=F32)
    copies[4].wait()
    source = source + jnp.dot(by_imag, pivot[1], preferred_element_type=F32)
    for d in range(LAST):
        t, i = divmod(d, FIVE)
        lanes = slice(LANES * t, LANES * (t + 1))
        pieces = [source[at : at + n, lanes] for at, n, _ in placed(DEEP * i, DEEP)]
        out[d] = jnp.concatenate(pieces + [fore[:, lanes], back[:, lanes]], axis=0)
    tiles = [slice(LANES * t, LANES * (t + 1)) for t in range(TILES)]
    last = HALF + HEAD
    pieces = [source[last - TAIL : last, lanes] for lanes in tiles]
    pieces += [fore[:, lanes] for lanes in tiles] + [back[:, lanes] for lanes in tiles]
    pieces += [jnp.zeros((16 - TILES * (TAIL + 2), LANES), F32)]
    out[LAST] = jnp.concatenate(pieces, axis=0)


def placed(start, count):
    if start >= HEAD:
        return [(start + PAD, count, 0)]
    ahead = min(count, HEAD - start)
    rest = [(HALF, count - ahead, ahead)] if ahead < count else []
    return [(start, ahead, 0)] + rest


def is_last():
    return lax.axis_index("hull") % GROUP == NEAR[LAST]


def spread(block, row, first, last):
    whole = jnp.broadcast_to(block[row : row + 1], (16, LANES))
    parts = [jnp.broadcast_to(block[first + t : first + t + 1], (TAIL, LANES)) for t in range(TILES)]
    parts.append(jnp.zeros((16 - TILES * TAIL, LANES), F32))
    return jnp.where(last, jnp.concatenate(parts, axis=0), whole)


def by_tile(matrix):
    return [matrix[TAIL * t : TAIL * t + 1] for t in range(TILES)]


def reduce_body(shares, picked, frequency, spectrum, out):
    last = is_last()
    got = [shares[NEAR.index(j)] for j in range(GROUP)]
    fores = [spread(block, DEEP, TILES * TAIL, last) for block in got]
    backs = [spread(block, DEEP + 1, TILES * TAIL + TILES, last) for block in got]
    front, gain = got[0], fores[0]
    fronts, gains = [front], [gain]
    for j in range(1, GROUP):
        front = got[j] + front * fores[j]
        gain = gain * fores[j]
        fronts.append(front)
        gains.append(gain)
    motion, through, back_gain = front, gain, backs[GROUP - 1]
    for j in range(GROUP - 2, -1, -1):
        motion = fronts[j] + motion * backs[j]
        through = gains[j] + through * backs[j]
        back_gain = back_gain * backs[j]

    def pack(third):
        whole = [front[0:DEEP], motion[0:DEEP], gain[0:1], third[0:1], back_gain[0:1]]
        whole.append(jnp.zeros((1, LANES), F32))
        some = TILES * TAIL
        parts = [front[0:some]] + by_tile(gain) + by_tile(third)
        parts += [jnp.zeros((DEEP - some - 2 * TILES, LANES), F32), motion[0:some]] + by_tile(back_gain)
        parts.append(jnp.zeros((ENDS - DEEP - some - TILES, LANES), F32))
        return jnp.where(last, jnp.concatenate(parts, axis=0), jnp.concatenate(whole, axis=0))

    ahead, aft = pack(backs[GROUP - 1]), pack(through)
    mine = lax.axis_index("hull") // GROUP
    for place in range(SPAN):
        out[place] = jnp.where(mine < FAR[place], ahead, aft)


def solve_body(shares, reached, out, into, beyond, before):
    mine = lax.axis_index("hull") // GROUP
    last = is_last()
    some = TILES * TAIL
    zero = jnp.zeros((16, LANES), F32)
    ends = [reached[FAR.index(g)] for g in range(SPAN)]
    thirds = [spread(block, 2 * DEEP + 1, some + TILES, last) for block in ends]
    into[0] = zero
    before[0] = zero
    arriving = [zero]
    for g in range(SPAN - 1):
        arriving.append(ends[g][0:16] + arriving[g] * spread(ends[g], 2 * DEEP, some, last))
        into[g + 1] = arriving[g + 1]
        before[g + 1] = thirds[g]
    returning = zero
    beyond[SPAN - 1] = zero
    for g in range(SPAN - 1, 0, -1):
        returning = (
            ends[g][DEEP : DEEP + 16]
            + arriving[g] * thirds[g]
            + returning * spread(ends[g], 2 * DEEP + 2, DEEP + some, last)
        )
        beyond[g - 1] = returning
    enter = into[mine]
    front = enter
    got = [shares[NEAR.index(j)] for j in range(GROUP)]
    fronts = []
    for j in range(GROUP):
        front = got[j] + front * spread(got[j], DEEP, some, last)
        fronts.append(front)
    motion = beyond[mine]
    motions = [None] * GROUP
    for j in range(GROUP - 1, -1, -1):
        motion = fronts[j] + motion * spread(got[j], DEEP + 1, some + TILES, last)
        motions[j] = motion
    previous = enter + motion * before[mine]
    for j in range(GROUP):
        both = jnp.concatenate([motions[j][0:DEEP], previous[0:DEEP]], axis=0)
        for q in range(2 * DEEP // 4):
            out[BACK.index(j), q] = both[4 * q : 4 * q + 4]
        previous = motions[j]


def split(values, parts):
    pieces = []
    for _ in range(parts):
        piece = values.astype(BF16)
        values = values - piece.astype(F32)
        pieces.append(piece)
    return jnp.concatenate(pieces, axis=0)


def pick_body(recovery, hotspots, picked):
    elements = lax.broadcasted_iota(jnp.int32, (POINTS, POINTS), 0)
    chosen = jnp.where(elements == hotspots[...], 1.0, 0.0).astype(BF16)
    contract = (((0,), (0,)), ((), ()))
    rows = lax.dot_general(chosen, recovery[0], contract, preferred_element_type=F32)
    picked[...] = rows.astype(BF16)


def stress_body(got, picked, frequency, spectrum, motion_out, out, motion, stern):
    for part in range(2):
        rows = slice(HALF * part + HEAD, HALF * (part + 1))
        motion[rows] = jnp.zeros((PAD, MODES), F32)
        stern[rows] = jnp.zeros((PAD, MODES), F32)
    for place in range(GROUP):
        d = NEAR.index(BACK[place])
        block = jnp.concatenate([got[place, q] for q in range(2 * DEEP // 4)], axis=0)
        t, i = divmod(d, FIVE)
        pieces = [(t, at, n, skip) for at, n, skip in placed(DEEP * i, DEEP)]
        if d == LAST:
            pieces = [(t, HALF + HEAD - TAIL, TAIL, TAIL * t) for t in range(TILES)]
        for t, at, n, skip in pieces:
            lanes = slice(LANES * t, LANES * (t + 1))
            motion[at : at + n, lanes] = block[skip : skip + n]
            stern[at : at + n, lanes] = block[DEEP + skip : DEEP + skip + n]
    motion_out[0, 0, :, 0, :] = motion[0:HEAD]
    motion_out[0, 0, :, 1, :] = motion[HALF : HALF + HEAD]
    contract = (((1,), (1,)), ((), ()))
    both = lax.dot_general(
        split(stern[...], 2), picked[:, 0:MODES], contract, preferred_element_type=F32
    ) + lax.dot_general(
        split(motion[...], 2), picked[:, MODES:], contract, preferred_element_type=F32
    )
    stress = both[0 : 2 * HALF] + both[2 * HALF :]
    power = stress[0:HALF] ** 2 + stress[HALF:] ** 2
    rows = lax.broadcasted_iota(jnp.int32, (HALF, HEAD), 0)
    columns = lax.broadcasted_iota(jnp.int32, (HALF, HEAD), 1)
    weight = jnp.sum(jnp.where(rows == columns, spectrum[...], 0.0), axis=1, keepdims=True)
    energy = power * (weight * (1.2 / 4))
    here = jnp.broadcast_to(frequency[...].reshape(1, 1), (1, POINTS))
    rows = lax.broadcasted_iota(jnp.int32, (HALF, POINTS), 0)
    packed = jnp.where(rows < HEAD, energy, here)
    for f in range(4):
        out[f] = packed


def damage_body(got, motion, moments_out, damage_out, motion_out, moments, damage, sent):
    copies = [
        pltpu.make_async_copy(motion, motion_out, sent.at[0]),
        pltpu.make_async_copy(moments, moments_out, sent.at[1]),
        pltpu.make_async_copy(damage, damage_out, sent.at[2]),
    ]
    copies[0].start()
    zeroth = jnp.zeros((HEAD, POINTS), F32)
    second = zeroth
    fourth = zeroth
    for f in range(4):
        energy = got[f, 0:HEAD]
        square = got[f, HEAD : HEAD + 1] ** 2
        zeroth = zeroth + energy
        second = second + energy * square
        fourth = fourth + energy * (square * square)
    moments[0, :, 0, :] = zeroth
    moments[1, :, 0, :] = second
    moments[2, :, 0, :] = fourth
    copies[1].start()
    damage[:, 0, :] = (
        0.5 * jnp.log(fourth / second)
        + 1.5 * jnp.log(zeroth)
        + jnp.log(0.5 + 0.5 * second / jnp.sqrt(zeroth * fourth))
    )
    copies[2].start()
    for copy in copies:
        copy.wait()


def exchange(values, axis, groups):
    return lax.all_to_all(values, axis, 0, 0, axis_index_groups=groups, tiled=True)


def per_device(wave_loads, pivot_inverse, forward, backward, recovery, hotspots, frequency, spectrum):
    near = [[GROUP * g + j for j in NEAR] for g in range(SPAN)]
    back = [[GROUP * g + j for j in BACK] for g in range(SPAN)]
    far = [[GROUP * g + j for g in FAR] for j in range(GROUP)]
    (source,) = call(
        source_body,
        [(GROUP, 16, LANES)],
        jnp.transpose(wave_loads, (0, 1, 3, 2, 4)),
        pivot_inverse,
        forward[0],
        backward[0],
        spaces=[pl.ANY] * 4,
        vmem_mib=56,
        scratch=[
            pltpu.VMEM((HEAD, 2, MODES), BF16),
            pltpu.VMEM((2, MODES, MODES), BF16),
            pltpu.VMEM((1, MODES), BF16),
            pltpu.VMEM((1, MODES), BF16),
            pltpu.SemaphoreType.DMA((5,)),
        ],
    )
    (picked,) = call(pick_body, [(POINTS, 2 * MODES)], recovery, hotspots, kind=BF16)
    shares = exchange(source, "hull", near)
    (ends,) = call(reduce_body, [(SPAN, ENDS, LANES)], shares, picked, frequency, spectrum)
    ends = exchange(ends, "hull", far)
    (solved,) = call(
        solve_body,
        [(GROUP, 2 * DEEP // 4, 4, LANES)],
        shares,
        ends,
        scratch=[pltpu.VMEM((SPAN, 16, LANES), F32)] * 3,
    )
    solved = exchange(solved, "hull", back)
    motion, energy = call(
        stress_body,
        [(1, 1, HEAD, 2, MODES), (4, HALF, POINTS)],
        solved,
        picked,
        frequency,
        spectrum,
        scratch=[pltpu.VMEM((2 * HALF, MODES), F32)] * 2,
    )
    energy = exchange(energy, "freq", [WAVES])
    shapes = [(3, HEAD, 1, POINTS), (HEAD, 1, POINTS)]
    moments, damage, motion = call(
        damage_body,
        shapes + [motion.shape],
        energy,
        motion,
        out_spaces=[pltpu.HBM] * 3,
        scratch=[pltpu.VMEM(shape, F32) for shape in shapes] + [pltpu.SemaphoreType.DMA((3,))],
    )
    return (
        jnp.transpose(motion, (0, 1, 3, 2, 4)),
        jnp.transpose(moments, (0, 2, 1, 3)),
        jnp.transpose(damage, (1, 0, 2)),
    )


def solution(mesh):
    in_specs = (
        P("freq", "hull", None, None, None),
        P("freq", "hull", None, None, None),
        P("freq", "hull", None),
        P("freq", "hull", None),
        P("hull", None, None),
        P("hull", None),
        P("freq"),
        P("freq", None),
    )
    out_specs = (
        P("freq", "hull", None, None, None),
        P(None, "hull", None, None),
        P("hull", None, None),
    )
    return jax.shard_map(per_device, mesh=mesh, in_specs=in_specs, out_specs=out_specs, check_vma=False)
```

```python
import jax
import jax.numpy as jnp
from jax import lax
from jax.experimental import pallas as pl
from jax.experimental.pallas import tpu as pltpu
from jax.sharding import PartitionSpec as P

SPAN, GROUP = 8, 16
HEAD, MODES, POINTS = 36, 384, 256
LANES = 128
TILES = MODES // LANES
HALF = 40
PAD = HALF - HEAD
DEEP, FIVE = 14, 5
TAIL = 2 * HEAD - DEEP * FIVE
LAST = FIVE * TILES
ENDS = 32
NEAR = (15, 14, 13, 12, 11, 10, 9, 8, 7, 6, 5, 4, 3, 2, 1, 0)
BACK = (15, 14, 13, 12, 11, 10, 9, 8, 7, 6, 5, 4, 3, 2, 1, 0)
FAR = (5, 0, 1, 2, 3, 4, 6, 7)
WAVES = (2, 0, 1, 3)
F32 = jnp.float32
BF16 = jnp.bfloat16


def call(body, shapes, *args, kind=F32, spaces=None, out_spaces=None, vmem_mib=12, scratch=()):
    outs = [jax.ShapeDtypeStruct(shape, kind) for shape in shapes]
    spaces = spaces or [pltpu.VMEM] * len(args)
    out_spaces = out_spaces or [pltpu.VMEM] * len(outs)
    return pl.pallas_call(
        body,
        out_shape=outs,
        in_specs=[pl.BlockSpec(memory_space=space) for space in spaces],
        out_specs=[pl.BlockSpec(memory_space=space) for space in out_spaces],
        scratch_shapes=list(scratch),
        compiler_params=pltpu.CompilerParams(vmem_limit_bytes=vmem_mib * 2**20),
    )(*args)


def padded(rows):
    return jnp.concatenate([rows, jnp.zeros((HALF - HEAD, rows.shape[1]), rows.dtype)], axis=0)


def source_body(loads_hbm, pivot_hbm, forward_hbm, backward_hbm, out, loads, pivot, forward, backward, arrived):
    copies = [
        pltpu.make_async_copy(loads_hbm.at[0, 0], loads, arrived.at[0]),
        pltpu.make_async_copy(forward_hbm, forward, arrived.at[1]),
        pltpu.make_async_copy(backward_hbm, backward, arrived.at[2]),
        pltpu.make_async_copy(pivot_hbm.at[0, 0, 0], pivot.at[0], arrived.at[3]),
        pltpu.make_async_copy(pivot_hbm.at[0, 0, 1], pivot.at[1], arrived.at[4]),
    ]
    for i in (3, 0, 4, 1, 2):
        copies[i].start()
    copies[0].wait()
    both = loads[...].astype(F32)
    real = padded(both[:, 0, :])
    imag = padded(both[:, 1, :])
    by_real = jnp.concatenate([real, imag], axis=0).astype(BF16)
    by_imag = jnp.concatenate([-imag, real], axis=0).astype(BF16)
    copies[1].wait()
    copies[2].wait()
    fore = -forward[...].astype(F32)
    back = -backward[...].astype(F32)
    copies[3].wait()
    source = jnp.dot(by_real, pivot[0], preferred_element_type=F32)
    copies[4].wait()
    source = source + jnp.dot(by_imag, pivot[1], preferred_element_type=F32)
    for d in range(LAST):
        t, i = divmod(d, FIVE)
        lanes = slice(LANES * t, LANES * (t + 1))
        pieces = [source[at : at + n, lanes] for at, n, _ in placed(DEEP * i, DEEP)]
        out[d] = jnp.concatenate(pieces + [fore[:, lanes], back[:, lanes]], axis=0)
    tiles = [slice(LANES * t, LANES * (t + 1)) for t in range(TILES)]
    last = HALF + HEAD
    pieces = [source[last - TAIL : last, lanes] for lanes in tiles]
    pieces += [fore[:, lanes] for lanes in tiles] + [back[:, lanes] for lanes in tiles]
    pieces += [jnp.zeros((16 - TILES * (TAIL + 2), LANES), F32)]
    out[LAST] = jnp.concatenate(pieces, axis=0)


def placed(start, count):
    if start >= HEAD:
        return [(start + PAD, count, 0)]
    ahead = min(count, HEAD - start)
    rest = [(HALF, count - ahead, ahead)] if ahead < count else []
    return [(start, ahead, 0)] + rest


def is_last():
    return lax.axis_index("hull") % GROUP == NEAR[LAST]


def spread(block, row, first, last):
    whole = jnp.broadcast_to(block[row : row + 1], (16, LANES))
    parts = [jnp.broadcast_to(block[first + t : first + t + 1], (TAIL, LANES)) for t in range(TILES)]
    parts.append(jnp.zeros((16 - TILES * TAIL, LANES), F32))
    return jnp.where(last, jnp.concatenate(parts, axis=0), whole)


def by_tile(matrix):
    return [matrix[TAIL * t : TAIL * t + 1] for t in range(TILES)]


def reduce_body(shares, picked, frequency, spectrum, out):
    last = is_last()
    got = [shares[NEAR.index(j)] for j in range(GROUP)]
    fores = [spread(block, DEEP, TILES * TAIL, last) for block in got]
    backs = [spread(block, DEEP + 1, TILES * TAIL + TILES, last) for block in got]
    front, gain = got[0], fores[0]
    fronts, gains = [front], [gain]
    for j in range(1, GROUP):
        front = got[j] + front * fores[j]
        gain = gain * fores[j]
        fronts.append(front)
        gains.append(gain)
    motion, through, back_gain = front, gain, backs[GROUP - 1]
    for j in range(GROUP - 2, -1, -1):
        motion = fronts[j] + motion * backs[j]
        through = gains[j] + through * backs[j]
        back_gain = back_gain * backs[j]

    def pack(third):
        whole = [front[0:DEEP], motion[0:DEEP], gain[0:1], third[0:1], back_gain[0:1]]
        whole.append(jnp.zeros((1, LANES), F32))
        some = TILES * TAIL
        parts = [front[0:some]] + by_tile(gain) + by_tile(third)
        parts += [jnp.zeros((DEEP - some - 2 * TILES, LANES), F32), motion[0:some]] + by_tile(back_gain)
        parts.append(jnp.zeros((ENDS - DEEP - some - TILES, LANES), F32))
        return jnp.where(last, jnp.concatenate(parts, axis=0), jnp.concatenate(whole, axis=0))

    ahead, aft = pack(backs[GROUP - 1]), pack(through)
    mine = lax.axis_index("hull") // GROUP
    for place in range(SPAN):
        out[place] = jnp.where(mine < FAR[place], ahead, aft)


def solve_body(shares, reached, out, into, beyond, before):
    mine = lax.axis_index("hull") // GROUP
    last = is_last()
    some = TILES * TAIL
    zero = jnp.zeros((16, LANES), F32)
    ends = [reached[FAR.index(g)] for g in range(SPAN)]
    thirds = [spread(block, 2 * DEEP + 1, some + TILES, last) for block in ends]
    into[0] = zero
    before[0] = zero
    arriving = [zero]
    for g in range(SPAN - 1):
        arriving.append(ends[g][0:16] + arriving[g] * spread(ends[g], 2 * DEEP, some, last))
        into[g + 1] = arriving[g + 1]
        before[g + 1] = thirds[g]
    returning = zero
    beyond[SPAN - 1] = zero
    for g in range(SPAN - 1, 0, -1):
        returning = (
            ends[g][DEEP : DEEP + 16]
            + arriving[g] * thirds[g]
            + returning * spread(ends[g], 2 * DEEP + 2, DEEP + some, last)
        )
        beyond[g - 1] = returning
    enter = into[mine]
    front = enter
    got = [shares[NEAR.index(j)] for j in range(GROUP)]
    fronts = []
    for j in range(GROUP):
        front = got[j] + front * spread(got[j], DEEP, some, last)
        fronts.append(front)
    motion = beyond[mine]
    motions = [None] * GROUP
    for j in range(GROUP - 1, -1, -1):
        motion = fronts[j] + motion * spread(got[j], DEEP + 1, some + TILES, last)
        motions[j] = motion
    previous = enter + motion * before[mine]
    for j in range(GROUP):
        both = jnp.concatenate([motions[j][0:DEEP], previous[0:DEEP]], axis=0)
        for q in range(2 * DEEP // 4):
            out[BACK.index(j), q] = both[4 * q : 4 * q + 4]
        previous = motions[j]


def split(values, parts):
    pieces = []
    for _ in range(parts):
        piece = values.astype(BF16)
        values = values - piece.astype(F32)
        pieces.append(piece)
    return jnp.concatenate(pieces, axis=0)


def pick_body(recovery, hotspots, picked):
    elements = lax.broadcasted_iota(jnp.int32, (POINTS, POINTS), 0)
    chosen = jnp.where(elements == hotspots[...], 1.0, 0.0).astype(BF16)
    contract = (((0,), (0,)), ((), ()))
    rows = lax.dot_general(chosen, recovery[0], contract, preferred_element_type=F32)
    picked[...] = rows.astype(BF16)


def stress_body(got, picked, frequency, spectrum, motion_out, out, motion, stern):
    for part in range(2):
        rows = slice(HALF * part + HEAD, HALF * (part + 1))
        motion[rows] = jnp.zeros((PAD, MODES), F32)
        stern[rows] = jnp.zeros((PAD, MODES), F32)
    for place in range(GROUP):
        d = NEAR.index(BACK[place])
        block = jnp.concatenate([got[place, q] for q in range(2 * DEEP // 4)], axis=0)
        t, i = divmod(d, FIVE)
        pieces = [(t, at, n, skip) for at, n, skip in placed(DEEP * i, DEEP)]
        if d == LAST:
            pieces = [(t, HALF + HEAD - TAIL, TAIL, TAIL * t) for t in range(TILES)]
        for t, at, n, skip in pieces:
            lanes = slice(LANES * t, LANES * (t + 1))
            motion[at : at + n, lanes] = block[skip : skip + n]
            stern[at : at + n, lanes] = block[DEEP + skip : DEEP + skip + n]
    motion_out[0, 0, :, 0, :] = motion[0:HEAD]
    motion_out[0, 0, :, 1, :] = motion[HALF : HALF + HEAD]
    contract = (((1,), (1,)), ((), ()))
    both = lax.dot_general(
        split(stern[...], 2), picked[:, 0:MODES], contract, preferred_element_type=F32
    ) + lax.dot_general(
        split(motion[...], 2), picked[:, MODES:], contract, preferred_element_type=F32
    )
    stress = both[0 : 2 * HALF] + both[2 * HALF :]
    power = stress[0:HALF] ** 2 + stress[HALF:] ** 2
    rows = lax.broadcasted_iota(jnp.int32, (HALF, HEAD), 0)
    columns = lax.broadcasted_iota(jnp.int32, (HALF, HEAD), 1)
    weight = jnp.sum(jnp.where(rows == columns, spectrum[...], 0.0), axis=1, keepdims=True)
    energy = power * (weight * (1.2 / 4))
    here = jnp.broadcast_to(frequency[...].reshape(1, 1), (1, POINTS))
    rows = lax.broadcasted_iota(jnp.int32, (HALF, POINTS), 0)
    packed = jnp.where(rows < HEAD, energy, here)
    for f in range(4):
        out[f] = packed


def damage_body(got, motion, moments_out, damage_out, motion_out, moments, damage, sent):
    copies = [
        pltpu.make_async_copy(motion, motion_out, sent.at[0]),
        pltpu.make_async_copy(moments, moments_out, sent.at[1]),
        pltpu.make_async_copy(damage, damage_out, sent.at[2]),
    ]
    copies[0].start()
    zeroth = jnp.zeros((HEAD, POINTS), F32)
    second = zeroth
    fourth = zeroth
    for f in range(4):
        energy = got[f, 0:HEAD]
        square = got[f, HEAD : HEAD + 1] ** 2
        zeroth = zeroth + energy
        second = second + energy * square
        fourth = fourth + energy * (square * square)
    moments[0, :, 0, :] = zeroth
    moments[1, :, 0, :] = second
    moments[2, :, 0, :] = fourth
    copies[1].start()
    damage[:, 0, :] = (
        0.5 * jnp.log(fourth / second)
        + 1.5 * jnp.log(zeroth)
        + jnp.log(0.5 + 0.5 * second / jnp.sqrt(zeroth * fourth))
    )
    copies[2].start()
    for copy in copies:
        copy.wait()


def exchange(values, axis, groups):
    return lax.all_to_all(values, axis, 0, 0, axis_index_groups=groups, tiled=True)


def per_device(wave_loads, pivot_inverse, forward, backward, recovery, hotspots, frequency, spectrum):
    near = [[GROUP * g + j for j in NEAR] for g in range(SPAN)]
    back = [[GROUP * g + j for j in BACK] for g in range(SPAN)]
    far = [[GROUP * g + j for g in FAR] for j in range(GROUP)]
    (source,) = call(
        source_body,
        [(GROUP, 16, LANES)],
        jnp.transpose(wave_loads, (0, 1, 3, 2, 4)),
        pivot_inverse,
        forward[0],
        backward[0],
        spaces=[pl.ANY] * 4,
        vmem_mib=56,
        scratch=[
            pltpu.VMEM((HEAD, 2, MODES), BF16),
            pltpu.VMEM((2, MODES, MODES), BF16),
            pltpu.VMEM((1, MODES), BF16),
            pltpu.VMEM((1, MODES), BF16),
            pltpu.SemaphoreType.DMA((5,)),
        ],
    )
    (picked,) = call(pick_body, [(POINTS, 2 * MODES)], recovery, hotspots, kind=BF16)
    shares = exchange(source, "hull", near)
    (ends,) = call(reduce_body, [(SPAN, ENDS, LANES)], shares, picked, frequency, spectrum)
    ends = exchange(ends, "hull", far)
    (solved,) = call(
        solve_body,
        [(GROUP, 2 * DEEP // 4, 4, LANES)],
        shares,
        ends,
        scratch=[pltpu.VMEM((SPAN, 16, LANES), F32)] * 3,
    )
    solved = exchange(solved, "hull", back)
    motion, energy = call(
        stress_body,
        [(1, 1, HEAD, 2, MODES), (4, HALF, POINTS)],
        solved,
        picked,
        frequency,
        spectrum,
        scratch=[pltpu.VMEM((2 * HALF, MODES), F32)] * 2,
    )
    energy = exchange(energy, "freq", [WAVES])
    shapes = [(3, HEAD, 1, POINTS), (HEAD, 1, POINTS)]
    moments, damage, motion = call(
        damage_body,
        shapes + [motion.shape],
        energy,
        motion,
        out_spaces=[pltpu.HBM] * 3,
        scratch=[pltpu.VMEM(shape, F32) for shape in shapes] + [pltpu.SemaphoreType.DMA((3,))],
    )
    return (
        jnp.transpose(motion, (0, 1, 3, 2, 4)),
        jnp.transpose(moments, (0, 2, 1, 3)),
        jnp.transpose(damage, (1, 0, 2)),
    )


def solution(mesh):
    in_specs = (
        P("freq", "hull", None, None, None),
        P("freq", "hull", None, None, None),
        P("freq", "hull", None),
        P("freq", "hull", None),
        P("hull", None, None),
        P("hull", None),
        P("freq"),
        P("freq", None),
    )
    out_specs = (
        P("freq", "hull", None, None, None),
        P(None, "hull", None, None),
        P("hull", None, None),
    )
    return jax.shard_map(per_device, mesh=mesh, in_specs=in_specs, out_specs=out_specs, check_vma=False)
```
